32 devices in a mesh: pop: 4 (over x, core), shard: 8 (over z, y).
Axes of the slice: x: 2, y: 2, z: 4, core: 2. Of those that a mesh axis runs over, the one named last changes fastest.
Arguments:
- tokens: bfloat16 [8, 480, 4096], P('pop'), may hold values from -6 to 6
- gate_weight_matrix: bfloat16 [4096, 14336], P('pop', 'shard'), may hold values from -0.09375 to 0.09375
- w_up: bfloat16 [4096, 14336], P('pop', 'shard'), may hold values from -0.09375 to 0.09375
- a_gate: bfloat16 [8, 4, 4096], P('pop'), may hold values from -5 to 5
- a_up: bfloat16 [8, 4, 4096], P('pop'), may hold values from -5 to 5
- gate_hidden_factors: bfloat16 [8, 4, 14336], P('pop', None, 'shard'), may hold values from -5 to 5
- up_hidden_factors: bfloat16 [8, 4, 14336], P('pop', None, 'shard'), may hold values from -5 to 5
- fitness: bfloat16 [8], P('pop'), may hold values from -1 to 1
- readout: float32 [14336], P('shard'), may hold values from -0.13363062 to 0.13363062
Outputs:
- scores: float32 [8, 480], P('pop')
- upd_gate: float32 [4096, 14336], P('pop', 'shard')
- up_update_direction: float32 [4096, 14336], P('pop', 'shard')
The draws below stay inside these ranges and needn't reach their ends.
All inputs are finite; a program needn't handle non-finite values.
Results may differ from the reference program's by a relative error of at most 0.0003.
Values may be sent and summed in bfloat16 or wider, within the bound.
No kernel may reach another device: no remote copies, remote signals or barrier semaphores. Data moves between devices by JAX's collectives and lax.ppermute only.
A program may use at most 128 MiB of HBM per device.

```python
import math
import jax
import jax.numpy as jnp
from jax import lax

D = 4096
F = 14336
RANK = 4
TOK = 480
MEMBERS = 8


def draw_readout(key, part):
    position = jnp.arange(F, dtype=jnp.float32) / F
    values = jnp.clip(jax.random.normal(key, (F,), jnp.float32), -4.0, 4.0) * jnp.power(3.0, position)
    return values / math.sqrt(F)


def levels(own_key, extent, cuts, least, high):
    gain = 1.0
    for axis_at, blocks in cuts:
        steps = jax.random.uniform(jax.random.fold_in(jax.random.fold_in(own_key, 6), axis_at), (blocks,), jnp.float32, least / len(cuts), high / len(cuts))
        gain = gain * jnp.repeat(jnp.exp(steps), extent[axis_at] // blocks).reshape((-1,) + (1,) * (len(extent) - 1 - axis_at))
    return gain


def gaussian(rng, extent, deviation, limit, cuts=(), held_as=jnp.bfloat16):
    factor_of = levels(rng, extent, cuts, -0.22, 0.18) if cuts else 1.0
    array = jax.random.normal(rng, extent, jnp.float32) * deviation * factor_of
    return jnp.minimum(jnp.maximum(array, -limit), limit).astype(held_as)


def setup_inputs(seed: int = 0) -> dict:
    streams_of = jax.random.split(jax.random.key(seed), 10)
    tokens = gaussian(streams_of[0], (MEMBERS, TOK, D), 1.0, 6.0, ((0, 4),))
    gate_weight_matrix = gaussian(streams_of[1], (D, F), D ** -0.5, 0.09375, ((0, 4), (1, 8)))
    w_up = gaussian(streams_of[2], (D, F), D ** -0.5, 0.09375, ((0, 4), (1, 8)))
    a_gate = gaussian(streams_of[3], (MEMBERS, RANK, D), 1.0, 5.0, ((0, 4),))
    a_up = gaussian(streams_of[4], (MEMBERS, RANK, D), 1.0, 5.0, ((0, 4),))
    gate_hidden_factors = gaussian(streams_of[5], (MEMBERS, RANK, F), 1.0, 5.0, ((0, 4), (2, 8)))
    up_hidden_factors = gaussian(streams_of[6], (MEMBERS, RANK, F), 1.0, 5.0, ((0, 4), (2, 8)))
    fitness = jnp.clip(jax.random.uniform(streams_of[7], (MEMBERS,), jnp.float32, -1.0, 1.0) * levels(streams_of[7], (MEMBERS,), ((0, 4),), -0.4, 0.0), -1.0, 1.0).astype(jnp.bfloat16)
    readout = draw_readout(jax.random.fold_in(streams_of[9], 71), 0)
    return dict(tokens=tokens, gate_weight_matrix=gate_weight_matrix, w_up=w_up, a_gate=a_gate, a_up=a_up, gate_hidden_factors=gate_hidden_factors, up_hidden_factors=up_hidden_factors, fitness=fitness, readout=readout)


def member_fitness_eval(operands, gate_weight_matrix, w_up, readout, noise_scale):
    member_tokens, row_gate, row_up, col_gate, col_up = operands
    gate_projected = jnp.dot(member_tokens, row_gate.T, preferred_element_type=jnp.float32)
    up_projected = jnp.dot(member_tokens, row_up.T, preferred_element_type=jnp.float32)
    gate_pre = jnp.dot(member_tokens, gate_weight_matrix, preferred_element_type=jnp.float32) + noise_scale * jnp.dot(gate_projected, col_gate.astype(jnp.float32), precision=lax.Precision.HIGHEST)
    up_pre = jnp.dot(member_tokens, w_up, preferred_element_type=jnp.float32) + noise_scale * jnp.dot(up_projected, col_up.astype(jnp.float32), precision=lax.Precision.HIGHEST)
    hidden = jax.nn.silu(gate_pre) * up_pre
    return jnp.dot(hidden, readout, precision=lax.Precision.HIGHEST)

def direction(row_factor, col_factor, weighting):
    left_side = (row_factor.astype(jnp.float32) * weighting[:, None, None]).reshape(-1, row_factor.shape[2])
    right_side = col_factor.astype(jnp.float32).reshape(-1, col_factor.shape[2])
    return lax.dot_general(left_side, right_side, (((0,), (0,)), ((), ())), precision=lax.Precision.HIGHEST)

def reference(tokens, gate_weight_matrix, w_up, a_gate, a_up, gate_hidden_factors, up_hidden_factors, fitness, readout):
    noise_scale = 0.25 / math.sqrt(D * RANK)
    scores = lax.map(lambda operands: member_fitness_eval(operands, gate_weight_matrix, w_up, readout, noise_scale), (tokens, a_gate, a_up, gate_hidden_factors, up_hidden_factors))
    weighting = fitness.astype(jnp.float32) / math.sqrt(MEMBERS * RANK)
    upd_gate = direction(a_gate, gate_hidden_factors, weighting)
    up_update_direction = direction(a_up, up_hidden_factors, weighting)
    return (scores, upd_gate, up_update_direction)
```

```python
import functools
import math

import jax
import jax.numpy as jnp
from jax import lax
from jax.experimental import pallas as pl
from jax.experimental.pallas import tpu as pltpu
from jax.sharding import PartitionSpec as P

F32 = jnp.float32
BF16 = jnp.bfloat16


def split3(value):
    top = lax.reduce_precision(value, 8, 7)
    rest = value - top
    middle = lax.reduce_precision(rest, 8, 7)
    return [term.astype(BF16) for term in (top, middle, rest - middle)]


def column_chunks(width):
    cuts, begin = [], 0
    while begin < width:
        size = min(256, width - begin)
        cuts.append((begin, size))
        begin += size
    return cuts


def line_sizes(total):
    outer = 4 if total % 4 == 0 else 1
    return outer, total // outer


def swap_pairs(total, partner):
    return [(index, partner(index)) for index in range(total)]


def line_gather(own, size, coord, permute):
    if size == 1:
        return [(own, coord)]
    if size == 2:
        return [(own, coord), (permute(own, lambda c: c ^ 1), coord ^ 1)]
    if size == 4:
        even = lambda c: c ^ 1
        odd = lambda c: 3 - c if c in (1, 2) else c
        edge = jnp.logical_or(coord == 0, coord == 3)
        first = permute(own, even)
        across = permute(own, odd)
        second = jnp.where(edge, permute(across, even), across)
        across = permute(first, odd)
        third = jnp.where(edge, permute(across, even), across)
        place = [
            jnp.where(coord == 0, a, jnp.where(coord == 1, b, jnp.where(coord == 2, c, d)))
            for a, b, c, d in ((1, 0, 3, 2), (2, 2, 1, 1), (3, 3, 0, 0))
        ]
        return [(own, coord)] + list(zip((first, second, third), place))
    return [
        (own if step == 0 else permute(own, lambda c, step=step: (c + step) % size), (coord + size - step) % size)
        for step in range(size)
    ]


def gated_scores(ids, chunks, groups, pairs, readout, rows_per_block):
    arrays, specs = [ids, readout], [pl.BlockSpec(memory_space=pltpu.SMEM), pl.BlockSpec(memory_space=pltpu.VMEM)]

    def add(array, space):
        for index, seen in enumerate(arrays):
            if seen is array:
                return index
        arrays.append(array)
        specs.append(pl.BlockSpec(memory_space=space))
        return len(arrays) - 1

    used_chunks = sorted({pair[1] for pair in pairs})
    used_groups = sorted({pair[0] for pair in pairs})
    model_width = rows_per_block * sum(1 for _ in chunks[0][2])
    chunk_refs = {
        j: [(add(array, pl.ANY), lane, place) for array, lane, place in chunks[j][2]] for j in used_chunks
    }
    group_refs, shapes, scratch = {}, [], []
    for g in used_groups:
        sources, tile, noise_rows, noise_cols = groups[g]
        group_refs[g] = (
            [(add(array, pl.ANY), place) for array, place in sources],
            tile,
            add(noise_rows, pltpu.VMEM),
            add(noise_cols, pltpu.VMEM),
        )
        shapes.append(jax.ShapeDtypeStruct((noise_rows.shape[0], tile), F32))
    copies = 0
    for g in used_groups:
        rows = groups[g][0][0][0].shape[0]
        scratch.append(pltpu.VMEM((rows, model_width), BF16))
        copies += len(groups[g][0])
    for j in used_chunks:
        scratch.append(pltpu.VMEM((model_width, 2 * chunks[j][1]), BF16))
        copies += len(chunks[j][2])
    scratch.append(pltpu.SemaphoreType.DMA((copies,)))
    inputs, outputs = len(arrays), len(shapes)

    def kernel(*refs):
        ids_ref, readout_ref = refs[0], refs[1]
        outs = dict(zip(used_groups, refs[inputs : inputs + outputs]))
        held = refs[inputs + outputs :]
        tokens = dict(zip(used_groups, held[: len(used_groups)]))
        weights = dict(zip(used_chunks, held[len(used_groups) : -1]))
        sems = held[-1]
        pending, count = {}, 0

        def fetch(key):
            nonlocal count
            if key in pending:
                return
            started = []
            if key[0] == "w":
                width = 2 * chunks[key[1]][1]
                for index, lane, place in chunk_refs[key[1]]:
                    first = pl.multiple_of(ids_ref[place] * rows_per_block, rows_per_block)
                    started.append(
                        pltpu.make_async_copy(
                            refs[index].at[:, pl.ds(lane, width)],
                            weights[key[1]].at[pl.ds(first, rows_per_block), :],
                            sems.at[count],
                        )
                    )
                    count += 1
            else:
                for index, place in group_refs[key[1]][0]:
                    source, target = refs[index], tokens[key[1]]
                    if place is not None:
                        lanes = source.shape[1]
                        target = target.at[:, pl.ds(pl.multiple_of(ids_ref[place] * lanes, lanes), lanes)]
                    started.append(pltpu.make_async_copy(source, target, sems.at[count]))
                    count += 1
            for copy in started:
                copy.start()
            pending[key] = started

        for g, j in pairs:
            fetch(("w", j))
            fetch(("t", g))
        fresh = set()
        for g, j in pairs:
            for key in (("w", j), ("t", g)):
                for copy in pending[key]:
                    copy.wait()
                pending[key] = []
            begin, size, _ = chunks[j]
            _, tile, noise_rows, noise_cols = group_refs[g]
            first = g not in fresh
            fresh.add(g)

            def step(t, carry, g=g, j=j, begin=begin, size=size, tile=tile, noise_rows=noise_rows, noise_cols=noise_cols, first=first):
                rows = pl.ds(pl.multiple_of(t * tile, 16), tile)
                total = jnp.dot(tokens[g][rows, :], weights[j][...], preferred_element_type=F32)
                total += lax.dot_general(
                    refs[noise_rows][t],
                    refs[noise_cols][:, 2 * begin : 2 * begin + 2 * size],
                    (((0,), (0,)), ((), ())),
                    preferred_element_type=F32,
                )
                gate, up = total[:, :size], total[:, size:]
                value = gate / (1.0 + jnp.exp(-gate)) * up * readout_ref[:, begin : begin + size]
                if size == 256:
                    value = value[:, :128] + value[:, 128:]
                line = jnp.sum(value.T, axis=0, keepdims=True)
                at = pl.ds(t, 1)
                outs[g][at, :] = line if first else outs[g][at, :] + line
                return carry

            lax.fori_loop(0, groups[g][2].shape[0], step, 0)

    flops = sum(4 * groups[g][0][0][0].shape[0] * model_width * chunks[j][1] for g, j in pairs)
    return dict(
        zip(
            used_groups,
            pl.pallas_call(
                kernel,
                out_shape=shapes,
                in_specs=specs,
                out_specs=[pl.BlockSpec(memory_space=pltpu.VMEM)] * len(shapes),
                scratch_shapes=scratch,
                compiler_params=pltpu.CompilerParams(vmem_limit_bytes=48 * 1024 * 1024),
                cost_estimate=pl.CostEstimate(flops=flops, bytes_accessed=8 * 1024 * 1024, transcendentals=0),
            )(*arrays),
        )
    )


def row_chunks(rows):
    last = rows // 5
    return [(0, rows - last, (rows - last) // 2), (rows - last, last, last)]


def body(
    pop_size,
    shard_size,
    tokens,
    gate_weight_matrix,
    w_up,
    a_gate,
    a_up,
    gate_hidden_factors,
    up_hidden_factors,
    fitness,
    readout,
):
    members, tok_count, model_width = tokens.shape
    rank = a_gate.shape[1]
    rows = members * tok_count
    block_rows, hidden = gate_weight_matrix.shape
    half = hidden // 2
    lo_size = pop_size // 2
    outer, inner = line_sizes(shard_size)
    noise_scale = 0.25 / math.sqrt(model_width * rank)
    pop, shard = lax.axis_index("pop"), lax.axis_index("shard")
    hi, lo = pop // lo_size, pop % lo_size
    flat = tokens.reshape(rows, model_width)
    chunks = column_chunks(half)

    across_pairs = [(p, (p + lo_size) % pop_size) for p in range(pop_size)]

    def across(value):
        return lax.ppermute(value, "pop", across_pairs)

    def along(value, step):
        pairs = [(p, p // lo_size * lo_size + (p + step) % lo_size) for p in range(pop_size)]
        return lax.ppermute(value, "pop", pairs)

    def outer_permute(value, target):
        return lax.ppermute(
            value, "shard", [(s, target(s // inner) * inner + s % inner) for s in range(shard_size)]
        )

    def inner_permute(value, target):
        return lax.ppermute(
            value, "shard", [(s, s // inner * inner + target(s % inner)) for s in range(shard_size)]
        )

    piece_width = model_width // shard_size
    cuts = row_chunks(rows)
    sent = [
        across(lax.dynamic_slice(flat, (begin, shard * piece_width), (size, piece_width))) for begin, size, _ in cuts
    ]

    def pick(which):
        start = which * half
        gate = lax.dynamic_slice_in_dim(gate_weight_matrix, start, half, 1)
        up = lax.dynamic_slice_in_dim(w_up, start, half, 1)
        return [
            jnp.concatenate([gate[:, begin : begin + size], up[:, begin : begin + size]], 1) for begin, size in chunks
        ]

    passed = [across(block) for block in pick(1 - hi)]
    kept = jnp.concatenate(pick(hi), 1)
    near = [along(kept, step) for step in range(1, lo_size)]
    far = [[block] + [along(block, step) for step in range(1, lo_size)] for block in passed]

    gathered = []
    for index, block in enumerate(sent):
        pieces = []
        if index == 0:
            for piece, z in line_gather(block, outer, shard // inner, outer_permute):
                for part, y in line_gather(piece, inner, shard % inner, inner_permute):
                    pieces.append((part, z * inner + y))
        else:
            for piece, y in line_gather(block, inner, shard % inner, inner_permute):
                for part, z in line_gather(piece, outer, shard // inner, outer_permute):
                    pieces.append((part, z * inner + y))
        gathered.append(pieces)

    places = [hi * lo_size + (lo + lo_size - step) % lo_size for step in range(lo_size)]
    places += [(1 - hi) * lo_size + (lo + lo_size - step) % lo_size for step in range(lo_size)]
    for pieces in gathered:
        places += [place for _, place in pieces]
    ids = jnp.stack([jnp.asarray(place, jnp.int32) for place in places])

    chunk_list = []
    for index, (begin, size) in enumerate(chunks):
        sources = [(kept, 2 * begin, 0)] + [(block, 2 * begin, 1 + n) for n, block in enumerate(near)]
        sources += [(block, 0, lo_size + n) for n, block in enumerate(far[index])]
        chunk_list.append((begin, size, sources))

    factors = jnp.concatenate([a_gate, a_up], 1)
    columns = jnp.concatenate([gate_hidden_factors, up_hidden_factors], 1)
    lines = 2 * members * rank
    projected = noise_scale * jnp.einsum("mrd,mtd->mrt", factors, tokens, preferred_element_type=F32)
    other_projected = across(projected)
    block_half = model_width // 2
    bundle = jnp.concatenate(
        [
            columns.reshape(lines, hidden),
            lax.dynamic_slice_in_dim(factors.reshape(lines, model_width), (1 - hi) * block_half, block_half, 1),
            jnp.broadcast_to(fitness[:, None], (members, 2 * rank * 128)).reshape(lines, 128),
        ],
        1,
    )
    other_bundle = across(bundle)
    other_columns = other_bundle[:, :hidden].reshape(members, 2 * rank, hidden)

    def noise_lines(value):
        same = jnp.eye(members, dtype=BF16)[None, :, None, :, None]
        terms = jnp.stack(split3(value))[:, :, :, None, :]
        return (terms * same).reshape(3 * lines, rows)

    def noise_columns(value):
        value = lax.dynamic_slice_in_dim(value, hi * half, half, 2)
        zero = jnp.zeros((members, rank, half), BF16)
        gate = jnp.concatenate([value[:, :rank], zero], 1).reshape(lines, half)
        up = jnp.concatenate([zero, value[:, rank:]], 1).reshape(lines, half)
        blocks = []
        for begin, size in chunks:
            blocks += [gate[:, begin : begin + size], up[:, begin : begin + size]]
        return jnp.tile(jnp.concatenate(blocks, 1), (3, 1))

    def tiled(value, tile):
        return value.reshape(value.shape[0], value.shape[1] // tile, tile).transpose(1, 0, 2)

    own_lines, other_lines = noise_lines(projected), noise_lines(other_projected)
    own_columns, far_columns = noise_columns(columns), noise_columns(other_columns)
    groups = [([(flat, None)], tok_count, tiled(own_lines, tok_count), own_columns)]
    at = 2 * lo_size
    for pieces, (begin, size, tile) in zip(gathered, cuts):
        sources = [(piece, at + n) for n, (piece, _) in enumerate(pieces)]
        at += len(pieces)
        groups.append((sources, tile, tiled(other_lines[:, begin : begin + size], tile), far_columns))
    half_readout = lax.dynamic_slice_in_dim(readout, hi * half, half, 0)[None, :]

    last = len(chunks) - 1
    plan = [[(0, j)] for j in range(last - 1)]
    plan.append([(0, last - 1)] + [(1, j) for j in range(last)])
    plan.append([(0, last), (1, last)] + [(2, j) for j in range(last + 1)])
    results = [
        gated_scores(ids, chunk_list, groups, pairs, half_readout, block_rows) for pairs in plan if pairs
    ]
    totals = [
        sum(result[g] for result in results if g in result).reshape(-1) for g in range(len(groups))
    ]
    own_total, other_total = totals[0], jnp.concatenate(totals[1:])

    scores = own_total + across(other_total)
    scores = scores + sum(inner_permute(scores, lambda c, s=s: (c + s) % inner) for s in range(1, inner))
    scores = scores + sum(outer_permute(scores, lambda c, s=s: (c + s) % outer) for s in range(1, outer))

    both = jnp.stack([bundle, other_bundle])
    heads = jnp.stack([both[:, :, :hidden], both[:, :, :hidden]])[0]
    marks = both[:, :, hidden + block_half :]
    factor_parts = jnp.stack(
        [
            lax.dynamic_slice_in_dim(factors.reshape(lines, model_width), hi * block_half, block_half, 1),
            other_bundle[:, hidden : hidden + block_half],
        ]
    )

    def packed(target):
        return jnp.concatenate(
            [heads, lax.dynamic_slice_in_dim(factor_parts, target * block_rows, block_rows, 2), marks], 2
        )

    every = [packed(lo)]
    for step in range(1, lo_size):
        every.append(along(packed((lo + step) % lo_size), step))
    every = jnp.stack(every).reshape(pop_size, members, 2, rank, hidden + block_rows + 128)
    weighting = every[..., -1:].astype(F32) / math.sqrt(pop_size * members * rank)

    def direction(kind):
        part = every[:, :, kind].reshape(pop_size * members * rank, -1)
        weight = weighting[:, :, kind].reshape(-1, 1)
        left = jnp.concatenate(split3(part[:, hidden : hidden + block_rows].astype(F32) * weight))
        right = jnp.tile(part[:, :hidden], (3, 1))
        return lax.dot_general(left, right, (((0,), (0,)), ((), ())), preferred_element_type=F32)

    return scores.reshape(members, tok_count), direction(0), direction(1)


def solution(mesh):
    placed = (
        P("pop", None, None),
        P("pop", "shard"),
        P("pop", "shard"),
        P("pop", None, None),
        P("pop", None, None),
        P("pop", None, "shard"),
        P("pop", None, "shard"),
        P("pop"),
        P("shard"),
    )
    return jax.shard_map(
        functools.partial(body, mesh.shape["pop"], mesh.shape["shard"]),
        mesh=mesh,
        in_specs=placed,
        out_specs=(P("pop", None), P("pop", "shard"), P("pop", "shard")),
        check_vma=False,
    )
```

```python
import functools
import math

import jax
import jax.numpy as jnp
from jax import lax
from jax.experimental import pallas as pl
from jax.experimental.pallas import tpu as pltpu
from jax.sharding import PartitionSpec as P

F32 = jnp.float32
BF16 = jnp.bfloat16
MIB = 1024 * 1024
VMEM_BYTES = 64 * MIB
SMALL = pl.CostEstimate(flops=1, bytes_accessed=1, transcendentals=0)


def split3(value):
    top = lax.reduce_precision(value, 8, 7)
    rest = value - top
    middle = lax.reduce_precision(rest, 8, 7)
    return [term.astype(BF16) for term in (top, middle, rest - middle)]


def column_chunks(width):
    cuts, begin = [], 0
    while begin < width:
        size = min(256, width - begin)
        cuts.append((begin, size))
        begin += size
    return cuts


def line_sizes(total):
    outer = 4 if total % 4 == 0 else 1
    return outer, total // outer


def swap_pairs(total, partner):
    return [(index, partner(index)) for index in range(total)]


def line_steps(own, size, coord, permute):
    if size != 4:
        for step in range(1, size):
            block = permute(own, lambda c, step=step: (c + step) % size)
            hold = yield
            yield hold(block), (coord + size - step) % size
        return
    even = lambda c: c ^ 1
    odd = lambda c: 3 - c if c in (1, 2) else None
    edge = jnp.logical_or(coord == 0, coord == 3)
    places = [
        jnp.where(coord == 0, a, jnp.where(coord == 1, b, jnp.where(coord == 2, c, d)))
        for a, b, c, d in ((1, 0, 3, 2), (2, 2, 1, 1), (3, 3, 0, 0))
    ]
    first, across = permute(own, even), permute(own, odd)
    hold = yield
    first, across = hold(first), hold(across)
    yield first, places[0]
    ahead, over = permute(across, even), permute(first, odd)
    hold = yield
    ahead, over = hold(ahead), hold(over)
    yield jnp.where(edge, ahead, across), places[1]
    ahead = permute(over, even)
    hold = yield
    yield jnp.where(edge, hold(ahead), over), places[2]


def line_gather(own, size, coord, permute):
    found, steps = [(own, coord)], line_steps(own, size, coord, permute)
    for _ in range(size - 1):
        next(steps)
        found.append(steps.send(lambda value: value))
    return found


def after(value, *others):
    anywhere = pl.BlockSpec(memory_space=pltpu.HBM)
    return pl.pallas_call(
        lambda *refs: None,
        out_shape=jax.ShapeDtypeStruct(value.shape, value.dtype),
        in_specs=[anywhere] * (1 + len(others)),
        out_specs=anywhere,
        input_output_aliases={0: 0},
        compiler_params=pltpu.CompilerParams(vmem_limit_bytes=VMEM_BYTES),
        cost_estimate=SMALL,
    )(value, *others)


def gated_scores(ids, chunks, own, blocks, parts, readout, waited=()):
    arrays, specs = [], []

    def add(array, space):
        for index, seen in enumerate(arrays):
            if seen is array:
                return index
        arrays.append(array)
        specs.append(pl.BlockSpec(memory_space=space))
        return len(arrays) - 1

    add(ids, pltpu.SMEM)
    add(readout, pltpu.VMEM)
    for array in waited:
        add(array, pltpu.HBM)
    lines = own[1].shape[1]
    tiles, tile, width = own[0].shape
    place_count, block_rows = blocks[1].shape[0], blocks[1].shape[2]
    chunk_rows = chunks[0][2][0][0].shape[0]
    sizes = sorted({size for _, size, _ in chunks}, reverse=True)
    used_chunks = sorted({j for part in parts for j in range(part[3], part[4])})
    used_tiles = sorted({t for part in parts if part[0] for t in range(part[1], part[2])})
    used_blocks = sorted({t for part in parts if not part[0] for t in range(part[1], part[2])})
    slots, scratch, shapes, copies = {}, [], [], 0
    size_at = {}
    for size in sizes:
        those = [j for j in used_chunks if chunks[j][1] == size]
        if those:
            size_at[size] = len(scratch)
            scratch.append(pltpu.VMEM((len(those), width, 2 * size), BF16))
            for slot, j in enumerate(those):
                slots[j] = slot
    chunk_refs = {j: [(add(source[0], pltpu.HBM),) + source[1:] for source in chunks[j][2]] for j in used_chunks}
    copies += sum(len(refs) for refs in chunk_refs.values())
    own_at = block_at = own_out = block_out = None
    if used_tiles:
        own_at, own_out = len(scratch), len(shapes)
        scratch.append(pltpu.VMEM((len(used_tiles), tile, width), BF16))
        shapes.append(jax.ShapeDtypeStruct((tiles, tile), F32))
        own_ref, own_lines, own_cols = add(own[0], pltpu.HBM), add(own[1], pltpu.VMEM), add(own[2], pltpu.VMEM)
        copies += len(used_tiles)
    if used_blocks:
        block_at, block_out = len(scratch), len(shapes)
        scratch.append(pltpu.VMEM((len(used_blocks), block_rows, width), BF16))
        shapes.append(jax.ShapeDtypeStruct((place_count, block_rows), F32))
        far_lines, far_cols = add(blocks[1], pltpu.VMEM), add(blocks[2], pltpu.VMEM)
        block_refs = {n: [(add(array, pltpu.HBM), place) for array, place in blocks[0][n][1]] for n in used_blocks}
        copies += sum(len(refs) for refs in block_refs.values())
    scratch.append(pltpu.SemaphoreType.DMA((copies,)))
    inputs, outputs = len(arrays), len(shapes)

    def kernel(*refs):
        ids_ref, readout_ref = refs[0], refs[1]
        outs, held = refs[inputs : inputs + outputs], refs[inputs + outputs :]
        sems = held[-1]
        pending, count = {}, 0

        def fetch(key):
            nonlocal count
            if key in pending:
                return
            pairs = []
            if key[0] == "chunk":
                target = held[size_at[chunks[key[1]][1]]].at[slots[key[1]]]
                for index, lane, shift, to, lanes, place in chunk_refs[key[1]]:
                    first = pl.multiple_of(ids_ref[place] * chunk_rows, chunk_rows)
                    if shift is not None:
                        lane = pl.multiple_of(ids_ref[shift] * 128 + lane, 128)
                    source = refs[index].at[:, pl.ds(lane, lanes)]
                    pairs.append((source, target.at[pl.ds(first, chunk_rows), pl.ds(to, lanes)]))
            elif key[0] == "own":
                pairs.append((refs[own_ref].at[key[1]], held[own_at].at[used_tiles.index(key[1])]))
            else:
                for index, place in block_refs[key[1]]:
                    lanes = refs[index].shape[1]
                    first = pl.multiple_of(ids_ref[place] * lanes, lanes)
                    target = held[block_at].at[used_blocks.index(key[1]), :, pl.ds(first, lanes)]
                    pairs.append((refs[index], target))
            pending[key] = []
            for source, target in pairs:
                pending[key].append(pltpu.make_async_copy(source, target, sems.at[count]))
                pending[key][-1].start()
                count += 1

        def keys(part):
            mine, begin, end, first, last = part
            found = [("chunk", j) for j in range(first, last)]
            return found + [("own" if mine else "block", n) for n in range(begin, end)]

        for part in parts[:2]:
            for key in keys(part):
                fetch(key)
        for out in outs:
            out[...] = jnp.zeros(out.shape, F32)
        for number, part in enumerate(parts):
            for key in keys(part):
                for copy in pending[key]:
                    copy.wait()
                pending[key] = []
            if number + 2 < len(parts):
                for key in keys(parts[number + 2]):
                    fetch(key)
            mine, begin, end, first, last = part
            size = chunks[first][1]
            span = last - first

            def step(n, carry, mine=mine, begin=begin, end=end, first=first, size=size, span=span):
                t, j = n // span, n % span
                weights = held[size_at[size]].at[slots[first] + j]
                if mine:
                    tokens = held[own_at].at[used_tiles.index(begin) + t]
                    noise, columns = refs[own_lines].at[begin + t], refs[own_cols]
                    out, row = outs[own_out], begin + t
                else:
                    tokens = held[block_at].at[used_blocks.index(begin) + t]
                    row = ids_ref[blocks[0][begin][0] + t]
                    noise, columns = refs[far_lines].at[row], refs[far_cols]
                    out = outs[block_out]
                total = jnp.dot(tokens[...], weights[...], preferred_element_type=F32)
                at = chunks[first][0] + j * size
                if size % 128 == 0:
                    at = pl.multiple_of(at, 128)
                total += lax.dot_general(
                    noise[...],
                    columns[:, pl.ds(2 * at, 2 * size)],
                    (((0,), (0,)), ((), ())),
                    preferred_element_type=F32,
                )
                gate, up = total[:, :size], total[:, size:]
                value = gate / (1.0 + jnp.exp(-gate)) * up * readout_ref[:, pl.ds(at, size)]
                if size == 256:
                    value = value[:, :128] + value[:, 128:]
                out[pl.ds(row, 1), :] += jnp.sum(value.T, axis=0, keepdims=True)
                return carry

            if (end - begin) * span == 1:
                step(0, 0)
            else:
                lax.fori_loop(0, (end - begin) * span, step, 0)

    results = pl.pallas_call(
        kernel,
        out_shape=shapes,
        in_specs=specs,
        out_specs=[pl.BlockSpec(memory_space=pltpu.VMEM)] * len(shapes),
        scratch_shapes=scratch,
        compiler_params=pltpu.CompilerParams(vmem_limit_bytes=VMEM_BYTES),
        cost_estimate=SMALL,
    )(*arrays)
    return (results[own_out] if used_tiles else None), (results[block_out] if used_blocks else None)


def noise_columns(gate, up, cuts):
    blocks = []
    for begin, size in cuts:
        blocks += [gate[:, begin : begin + size], up[:, begin : begin + size]]
    value = jnp.concatenate(blocks, 1).astype(BF16)
    return jnp.concatenate([value] * 3, 0)


def own_factors(tokens, a_gate, a_up, gate_cols, up_cols, gate_half, up_half, marks, start, scale, cuts, waited):
    members, tok_count, width = tokens.shape
    rank, hidden, half = a_gate.shape[1], gate_cols.shape[2], gate_half.shape[2]
    lines, block_half = 2 * members * rank, width // 2

    def kernel(start_ref, tok_ref, ag, au, gc, uc, gh, uh, marks_ref, waited_ref, bundle, rows, cols):
        def both(gate, up):
            found = []
            for m in range(members):
                found += [gate(m).astype(F32), up(m).astype(F32)]
            return jnp.concatenate(found, 0).astype(BF16)

        bundle[:, :hidden] = both(lambda m: gc[m], lambda m: uc[m])
        lanes = pl.ds(pl.multiple_of(start_ref[0] * 128, 128), block_half)
        bundle[:, hidden : hidden + block_half] = both(lambda m: ag[m, :, lanes], lambda m: au[m, :, lanes])
        bundle[:, hidden + block_half : hidden + block_half + 128] = marks_ref[...]
        terms = []
        for m in range(members):
            factors = jnp.concatenate([ag[m].astype(F32), au[m].astype(F32)], 0).astype(BF16)
            value = scale * lax.dot_general(
                factors, tok_ref[m], (((1,), (1,)), ((), ())), preferred_element_type=F32
            )
            found = []
            for _ in range(3):
                found.append(value.astype(BF16).astype(F32))
                value = value - found[-1]
            terms.append(found)
            zero = jnp.zeros_like(value)
            lines_of = [found[n] if other == m else zero for n in range(3) for other in range(members)]
            rows[m] = jnp.concatenate(lines_of, 0).astype(BF16)
        ends = jnp.concatenate([jnp.concatenate(found, 1) for found in terms], 0)
        bundle[:, hidden + block_half + 128 :] = ends.astype(BF16)
        gates, ups = [], []
        for m in range(members):
            gate, up = gh[m].astype(F32), uh[m].astype(F32)
            gates += [gate, jnp.zeros_like(gate)]
            ups += [jnp.zeros_like(up), up]
        cols[...] = noise_columns(jnp.concatenate(gates, 0), jnp.concatenate(ups, 0), cuts)

    vmem = pl.BlockSpec(memory_space=pltpu.VMEM)
    return pl.pallas_call(
        kernel,
        out_shape=[
            jax.ShapeDtypeStruct((lines, hidden + block_half + 128 + 3 * tok_count), BF16),
            jax.ShapeDtypeStruct((members, 3 * lines, tok_count), BF16),
            jax.ShapeDtypeStruct((3 * lines, 2 * half), BF16),
        ],
        in_specs=[pl.BlockSpec(memory_space=pltpu.SMEM)] + [vmem] * 8 + [pl.BlockSpec(memory_space=pltpu.HBM)],
        out_specs=[vmem] * 3,
        compiler_params=pltpu.CompilerParams(vmem_limit_bytes=VMEM_BYTES),
        cost_estimate=SMALL,
    )(start, tokens, a_gate, a_up, gate_cols, up_cols, gate_half, up_half, marks, waited)


def other_factors(bundle, half_cols, first, members, tok_count, tile, cuts):
    lines, half = half_cols.shape
    rank = lines // members // 2
    count = members * tok_count // tile

    def kernel(bundle_ref, half_ref, rows, cols):
        for block in range(count):
            m, at = block * tile // tok_count, block * tile % tok_count
            found = []
            for n in range(3):
                lane = first + n * tok_count + at
                value = bundle_ref[:, lane : lane + tile].astype(F32)
                line = lax.broadcasted_iota(jnp.int32, value.shape, 0)
                found.append(jnp.where(line // (2 * rank) == m, value, 0.0))
            rows[block] = jnp.concatenate(found, 0).astype(BF16)
        value = half_ref[...].astype(F32)
        is_gate = lax.broadcasted_iota(jnp.int32, value.shape, 0) % (2 * rank) < rank
        cols[...] = noise_columns(jnp.where(is_gate, value, 0.0), jnp.where(is_gate, 0.0, value), cuts)

    vmem = pl.BlockSpec(memory_space=pltpu.VMEM)
    return pl.pallas_call(
        kernel,
        out_shape=[
            jax.ShapeDtypeStruct((count, 3 * lines, tile), BF16),
            jax.ShapeDtypeStruct((3 * lines, 2 * half), BF16),
        ],
        in_specs=[vmem] * 2,
        out_specs=[vmem] * 2,
        compiler_params=pltpu.CompilerParams(vmem_limit_bytes=VMEM_BYTES),
        cost_estimate=SMALL,
    )(bundle, half_cols)


def cut_blocks(gate, up, shift, cuts, waited):
    rows = gate.shape[0]

    def kernel(shift_ref, gate_ref, up_ref, waited_ref, *refs):
        blocks, held, sems = refs[: len(cuts)], refs[len(cuts) : -1], refs[-1]
        first, second = [], []
        for n, (begin, size) in enumerate(cuts):
            lanes = pl.ds(pl.multiple_of(shift_ref[0] * 128 + begin, 128), size)
            first.append([])
            for kind, source in enumerate((gate_ref, up_ref)):
                target = held[n].at[:, pl.ds(kind * size, size)]
                first[n].append(pltpu.make_async_copy(source.at[:, lanes], target, sems.at[3 * n + kind]))
                first[n][kind].start()
            second.append(pltpu.make_async_copy(held[n], blocks[n], sems.at[3 * n + 2]))
        for n in range(len(cuts)):
            for copy in first[n]:
                copy.wait()
            second[n].start()
        for copy in second:
            copy.wait()

    anywhere = pl.BlockSpec(memory_space=pltpu.HBM)
    return pl.pallas_call(
        kernel,
        out_shape=[jax.ShapeDtypeStruct((rows, 2 * size), gate.dtype) for _, size in cuts],
        in_specs=[pl.BlockSpec(memory_space=pltpu.SMEM), anywhere, anywhere, anywhere],
        out_specs=[anywhere] * len(cuts),
        scratch_shapes=[pltpu.VMEM((rows, 2 * size), gate.dtype) for _, size in cuts]
        + [pltpu.SemaphoreType.DMA((3 * len(cuts),))],
        compiler_params=pltpu.CompilerParams(vmem_limit_bytes=VMEM_BYTES),
        cost_estimate=SMALL,
    )(shift, gate, up, waited)


def body(
    pop_size,
    shard_size,
    tokens,
    gate_weight_matrix,
    w_up,
    a_gate,
    a_up,
    gate_hidden_factors,
    up_hidden_factors,
    fitness,
    readout,
):
    members, tok_count, model_width = tokens.shape
    rank = a_gate.shape[1]
    rows = members * tok_count
    block_rows, hidden = gate_weight_matrix.shape
    half = hidden // 2
    lo_size = pop_size // 2
    outer, inner = line_sizes(shard_size)
    noise_scale = 0.25 / math.sqrt(model_width * rank)
    pop, shard = lax.axis_index("pop"), lax.axis_index("shard")
    hi, lo = pop // lo_size, pop % lo_size
    flat = tokens.reshape(rows, model_width)
    chunks = column_chunks(half)

    across_pairs = [(p, (p + lo_size) % pop_size) for p in range(pop_size)]

    def across(value):
        return lax.ppermute(value, "pop", across_pairs)

    def along(value, step):
        pairs = [(p, p // lo_size * lo_size + (p + step) % lo_size) for p in range(pop_size)]
        return lax.ppermute(value, "pop", pairs)

    def outer_permute(value, target):
        pairs = [(s, target(s // inner), s % inner) for s in range(shard_size)]
        return lax.ppermute(value, "shard", [(s, z * inner + y) for s, z, y in pairs if z is not None])

    def inner_permute(value, target):
        pairs = [(s, s // inner, target(s % inner)) for s in range(shard_size)]
        return lax.ppermute(value, "shard", [(s, z * inner + y) for s, z, y in pairs if y is not None])

    z, y = shard // inner, shard % inner
    size_z, size_y = rows // outer, model_width // inner
    block = lax.dynamic_slice(flat, (z * size_z, y * size_y), (size_z, size_y))
    sent = across(block)

    lines = 2 * members * rank
    block_half = model_width // 2
    marks = jnp.broadcast_to(fitness[:, None], (members, 2 * rank * 128)).reshape(lines, 128)

    def in_half(value):
        return lax.dynamic_slice_in_dim(value, hi * half, half, value.ndim - 1)

    bundle, own_lines, own_columns = own_factors(
        tokens,
        a_gate,
        a_up,
        gate_hidden_factors,
        up_hidden_factors,
        in_half(gate_hidden_factors),
        in_half(up_hidden_factors),
        marks,
        ((1 - hi) * (block_half // 128)).astype(jnp.int32)[None],
        noise_scale,
        chunks,
        block,
    )
    other_bundle = across(bundle)
    bundle_width = hidden + block_half + 128

    def pick(which):
        if half % 128 == 0:
            shift = (which * (half // 128)).astype(jnp.int32)[None]
            return cut_blocks(gate_weight_matrix, w_up, shift, chunks, bundle)
        gate = lax.dynamic_slice_in_dim(gate_weight_matrix, which * half, half, 1)
        up = lax.dynamic_slice_in_dim(w_up, which * half, half, 1)
        return [
            jnp.concatenate([gate[:, begin : begin + size], up[:, begin : begin + size]], 1) for begin, size in chunks
        ]

    cut = pick(1 - hi)
    if half % 128 == 0:
        near = [(along(gate_weight_matrix, step), along(w_up, step)) for step in range(1, lo_size)]
        near = [(gate_weight_matrix, w_up)] + near
    else:
        kept = jnp.concatenate(pick(hi), 1)
        near = [kept] + [along(kept, step) for step in range(1, lo_size)]

    sent = after(sent, *cut, *jax.tree.leaves(near[1:]))
    other_bundle = after(other_bundle, sent)

    both = jnp.stack([bundle[:, :bundle_width], other_bundle[:, :bundle_width]])
    heads = both[:, :, :hidden]
    marks = both[:, :, hidden + block_half :]
    factors = jnp.concatenate([a_gate, a_up], 1)
    factor_parts = jnp.stack(
        [
            lax.dynamic_slice_in_dim(factors.reshape(lines, model_width), hi * block_half, block_half, 1),
            other_bundle[:, hidden : hidden + block_half],
        ]
    )

    def packed(target):
        return jnp.concatenate(
            [heads, lax.dynamic_slice_in_dim(factor_parts, target * block_rows, block_rows, 2), marks], 2
        )

    every = [packed(lo)]
    for step in range(1, lo_size):
        every.append(along(packed((lo + step) % lo_size), step))
    every = jnp.stack(every).reshape(pop_size, members, 2, rank, hidden + block_rows + 128)
    weighting = every[..., -1:].astype(F32) / math.sqrt(pop_size * members * rank)

    def direction(kind):
        part = every[:, :, kind].reshape(pop_size * members * rank, -1)
        weight = weighting[:, :, kind].reshape(-1, 1)
        left = jnp.concatenate(split3(part[:, hidden : hidden + block_rows].astype(F32) * weight))
        right = jnp.tile(part[:, :hidden], (3, 1))
        return lax.dot_general(left, right, (((0,), (0,)), ((), ())), preferred_element_type=F32)

    directions = [direction(0), direction(1)]

    far_lines, far_columns = other_factors(
        other_bundle, in_half(other_bundle[:, :hidden]), bundle_width, members, tok_count, size_z, chunks
    )
    half_readout = lax.dynamic_slice_in_dim(readout, hi * half, half, 0)[None, :]
    own = (tokens, own_lines, own_columns)
    held_at = pop_size + 1
    part_at = held_at + outer

    steps = line_steps(sent, outer, z, outer_permute)
    held, spread, far, chunk_list = [(sent, z)], [line_gather(sent, inner, y, inner_permute)], [], []
    end = len(chunks)
    passed = [across(cut[0])] + [None] * (end - 1)
    own_total = other_total = 0.0
    done, barrier = [0] * outer, list(directions)

    def gather_next():
        next(steps)
        held.append(steps.send(lambda value: after(value, *barrier)))
        spread.append(line_gather(held[-1][0], inner, y, inner_permute))

    def bring(j):
        if passed[j] is None:
            passed[j] = across(after(cut[j], *(far[j - 2] if j > 1 else [every])))
        return passed[j]

    def score(parts):
        nonlocal own_total, other_total
        places = [hi * lo_size + (lo + lo_size - step) % lo_size for step in range(lo_size)]
        places += [(1 - hi) * lo_size + (lo + lo_size - step) % lo_size for step in range(lo_size)]
        places += [hi * (half // 128)]
        places += [held[n][1] if n < len(held) else 0 for n in range(outer)] + [place for _, place in spread[0]]
        ids = jnp.stack([jnp.asarray(place, jnp.int32) for place in places])
        blocks = [
            (held_at + n, [(piece, part_at + k) for k, (piece, _) in enumerate(pieces)])
            for n, pieces in enumerate(spread)
        ]
        mine, theirs = gated_scores(
            ids, chunk_list, own, (blocks, far_lines, far_columns), parts, half_readout
        )
        own_total = own_total if mine is None else own_total + mine.reshape(-1)
        other_total = other_total if theirs is None else other_total + theirs.reshape(-1)
        return [value for value in (mine, theirs) if value is not None]

    for j in range(end):
        block = bring(j)
        if len(held) < outer:
            recent = spread[-1][-1][0]
            gather_next()
            block = after(block, held[-1][0], recent)
        elif j:
            block = after(block, *barrier)
        far.append([block] + [along(block, step) for step in range(1, lo_size)])
        begin, size = chunks[j]
        sources = []
        for n, kept_block in enumerate(near):
            if half % 128 == 0:
                sources += [(value, begin, pop_size, k * size, size, n) for k, value in enumerate(kept_block)]
            else:
                sources.append((kept_block, 2 * begin, None, 0, 2 * size, n))
        sources += [(value, 0, None, 0, 2 * size, lo_size + n) for n, value in enumerate(far[j])]
        chunk_list.append((begin, size, sources))
        parts = [(True, t, t + 1, j, j + 1) for t in range(members)]
        for n in range(min(j, outer)):
            parts += [(False, n, n + 1, i, i + 1) for i in range(done[n], j + 1)]
            done[n] = j + 1
        barrier = score(parts)
    while len(held) < outer:
        gather_next()
    score([(False, n, n + 1, i, i + 1) for n in range(outer) for i in range(done[n], end)])

    scores = own_total + across(other_total)
    scores = scores + sum(inner_permute(scores, lambda c, s=s: (c + s) % inner) for s in range(1, inner))
    scores = scores + sum(outer_permute(scores, lambda c, s=s: (c + s) % outer) for s in range(1, outer))

    return scores.reshape(members, tok_count), directions[0], directions[1]


def solution(mesh):
    placed = (
        P("pop", None, None),
        P("pop", "shard"),
        P("pop", "shard"),
        P("pop", None, None),
        P("pop", None, None),
        P("pop", None, "shard"),
        P("pop", None, "shard"),
        P("pop"),
        P("shard"),
    )
    return jax.shard_map(
        functools.partial(body, mesh.shape["pop"], mesh.shape["shard"]),
        mesh=mesh,
        in_specs=placed,
        out_specs=(P("pop", None), P("pop", "shard"), P("pop", "shard")),
        check_vma=False,
    )
```

```python
import functools
import math

import jax
import jax.numpy as jnp
from jax import lax
from jax.experimental import pallas as pl
from jax.experimental.pallas import tpu as pltpu
from jax.sharding import PartitionSpec as P

F32 = jnp.float32
BF16 = jnp.bfloat16
MIB = 1024 * 1024
VMEM_BYTES = 64 * MIB
SMALL = pl.CostEstimate(flops=1, bytes_accessed=1, transcendentals=0)


def split3(value):
    top = lax.reduce_precision(value, 8, 7)
    rest = value - top
    middle = lax.reduce_precision(rest, 8, 7)
    return [term.astype(BF16) for term in (top, middle, rest - middle)]


def column_chunks(width):
    return [[(begin, min(256, width - begin))] for begin in range(0, width, 256)]


def line_sizes(total):
    outer = 4 if total % 4 == 0 else 1
    return outer, total // outer


def swap_pairs(total, partner):
    return [(index, partner(index)) for index in range(total)]


def line_steps(own, size, coord, permute):
    if size != 4:
        for step in range(1, size):
            block = permute(own, lambda c, step=step: (c + step) % size)
            hold = yield
            yield hold(block)
        return
    even = lambda c: c ^ 1
    odd = lambda c: 3 - c if c in (1, 2) else None
    edge = jnp.logical_or(coord == 0, coord == 3)
    first, across = permute(own, even), permute(own, odd)
    hold = yield
    first, across = hold(first), hold(across)
    yield first
    ahead, over = permute(across, even), permute(first, odd)
    hold = yield
    ahead, over = hold(ahead), hold(over)
    yield jnp.where(edge, ahead, across)
    ahead = permute(over, even)
    hold = yield
    yield jnp.where(edge, hold(ahead), over)


def line_places(size, coord):
    if size != 4:
        return [coord] + [(coord + size - step) % size for step in range(1, size)]
    return [coord] + [
        jnp.where(coord == 0, a, jnp.where(coord == 1, b, jnp.where(coord == 2, c, d)))
        for a, b, c, d in ((1, 0, 3, 2), (2, 2, 1, 1), (3, 3, 0, 0))
    ]


def line_gather(own, size, coord, permute):
    found, steps = [own], line_steps(own, size, coord, permute)
    for _ in range(size - 1):
        next(steps)
        found.append(steps.send(lambda value: value))
    return found


def after(value, *others):
    anywhere = pl.BlockSpec(memory_space=pltpu.HBM)
    return pl.pallas_call(
        lambda *refs: None,
        out_shape=jax.ShapeDtypeStruct(value.shape, value.dtype),
        in_specs=[anywhere] * (1 + len(others)),
        out_specs=anywhere,
        input_output_aliases={0: 0},
        compiler_params=pltpu.CompilerParams(vmem_limit_bytes=VMEM_BYTES),
        cost_estimate=SMALL,
    )(value, *others)


def gated_scores(ids, chunks, own, blocks, parts, readout):
    arrays, specs, scratch, shapes, copies = [], [], [], [], 0

    def add(array, space):
        for index, seen in enumerate(arrays):
            if seen is array:
                return index
        arrays.append(array)
        specs.append(pl.BlockSpec(memory_space=space))
        return len(arrays) - 1

    add(ids, pltpu.SMEM)
    small = []

    def add_small(array):
        small.append((add(array, pltpu.HBM), len(scratch)))
        scratch.append(pltpu.VMEM(array.shape, array.dtype))
        return small[-1][1]

    lines = own[1].shape[1]
    tiles, tile, width = own[0].shape
    place_count, block_rows = blocks[1].shape[0], blocks[1].shape[2]
    chunk_rows = chunks[0][2][0][0].shape[0]
    used_chunks = sorted({j for part in parts for j in range(part[3], part[4])})
    used_tiles = sorted({t for part in parts if part[0] for t in range(part[1], part[2])})
    used_blocks = sorted({t for part in parts if not part[0] for t in range(part[1], part[2])})
    lane_at, total_lanes = {}, 0
    for j in used_chunks:
        lane_at[j] = total_lanes
        total_lanes += 2 * chunks[j][1]
    weights_at = len(scratch)
    scratch.append(pltpu.VMEM((width, total_lanes), BF16))
    chunk_refs = {j: [(add(source[0], pltpu.HBM),) + source[1:] for source in chunks[j][2]] for j in used_chunks}
    copies += sum(len(refs) for refs in chunk_refs.values())
    own_at = block_at = own_out = block_out = None
    if used_tiles:
        own_at, own_out = len(scratch), len(shapes)
        scratch.append(pltpu.VMEM((len(used_tiles) * tile, width), BF16))
        shapes.append(jax.ShapeDtypeStruct((tiles, tile), F32))
        own_ref, own_lines, own_cols = add(own[0], pltpu.HBM), add_small(own[1]), add_small(own[2])
        copies += len(used_tiles)
    if used_blocks:
        block_at, block_out = len(scratch), len(shapes)
        scratch.append(pltpu.VMEM((len(used_blocks) * block_rows, width), BF16))
        shapes.append(jax.ShapeDtypeStruct((place_count, block_rows), F32))
        far_lines, far_cols = add_small(blocks[1]), add_small(blocks[2])
        block_refs = {n: [(add(array, pltpu.HBM), place) for array, place in blocks[0][n][1]] for n in used_blocks}
        copies += sum(len(refs) for refs in block_refs.values())
    readout_at = add_small(readout)
    scratch.append(pltpu.SemaphoreType.DMA((copies + len(small),)))
    inputs, outputs = len(arrays), len(shapes)

    def kernel(*refs):
        ids_ref = refs[0]
        outs, held = refs[inputs : inputs + outputs], refs[inputs + outputs :]
        sems, readout_ref = held[-1], held[readout_at]
        pending, count = {}, 0

        def fetch(key):
            nonlocal count
            if key in pending:
                return
            pairs = []
            if key[0] == "chunk":
                for index, lane, shift, to, lanes, place in chunk_refs[key[1]]:
                    first = pl.multiple_of(ids_ref[place] * chunk_rows, chunk_rows)
                    if shift is not None:
                        lane = pl.multiple_of(ids_ref[shift] * 128 + lane, 128)
                    source = refs[index].at[:, pl.ds(lane, lanes)]
                    target = held[weights_at].at[pl.ds(first, chunk_rows), pl.ds(lane_at[key[1]] + to, lanes)]
                    pairs.append((source, target))
            elif key[0] == "own":
                rows = pl.ds(used_tiles.index(key[1]) * tile, tile)
                pairs.append((refs[own_ref].at[key[1]], held[own_at].at[rows, :]))
            else:
                for index, place in block_refs[key[1]]:
                    lanes = refs[index].shape[1]
                    first = pl.multiple_of(ids_ref[place] * lanes, lanes)
                    rows = pl.ds(used_blocks.index(key[1]) * block_rows, block_rows)
                    target = held[block_at].at[rows, pl.ds(first, lanes)]
                    pairs.append((refs[index], target))
            pending[key] = []
            for source, target in pairs:
                pending[key].append(pltpu.make_async_copy(source, target, sems.at[count]))
                pending[key][-1].start()
                count += 1

        def keys(part):
            mine, begin, end, first, last = part
            found = [("chunk", j) for j in range(first, last)]
            return found + [("own" if mine else "block", n) for n in range(begin, end)]

        first_copies = []
        for n, (index, place) in enumerate(small):
            first_copies.append(pltpu.make_async_copy(refs[index], held[place], sems.at[copies + n]))
            first_copies[-1].start()
        for part in parts[:2]:
            for key in keys(part):
                fetch(key)
        for out in outs:
            out[...] = jnp.zeros(out.shape, F32)
        for copy in first_copies:
            copy.wait()
        for number, part in enumerate(parts):
            for key in keys(part):
                for copy in pending[key]:
                    copy.wait()
                pending[key] = []
            if number + 2 < len(parts):
                for key in keys(parts[number + 2]):
                    fetch(key)
            mine, begin, end, first, last = part
            if mine:
                held_rows, height, at = held[own_at], tile, used_tiles.index(begin)
            else:
                held_rows, height, at = held[block_at], block_rows, used_blocks.index(begin)
            lanes = slice(lane_at[first], lane_at[last - 1] + 2 * chunks[last - 1][1])
            top, tall = at * height, (end - begin) * height
            piece = 240 if lanes.stop - lanes.start <= 256 and tall % 240 == 0 else tall
            pieces = [
                jnp.dot(held_rows[top + k : top + k + piece, :], held[weights_at][:, lanes], preferred_element_type=F32)
                for k in range(0, tall, piece)
            ]
            total = jnp.concatenate(pieces, 0) if len(pieces) > 1 else pieces[0]
            for t in range(end - begin):
                if mine:
                    row, noise, columns = begin + t, held[own_lines].at[begin + t], held[own_cols]
                else:
                    row = ids_ref[blocks[0][begin + t][0]]
                    noise, columns = held[far_lines].at[row], held[far_cols]
                begin_lane = 2 * chunks[first][0]
                part_total = total[t * height : (t + 1) * height, :] + lax.dot_general(
                    noise[...],
                    columns[:, begin_lane : begin_lane + lanes.stop - lanes.start],
                    (((0,), (0,)), ((), ())),
                    preferred_element_type=F32,
                )
                line = 0.0
                for j in range(first, last):
                    start, size, _ = chunks[j]
                    lane = lane_at[j] - lane_at[first]
                    gate, up = part_total[:, lane : lane + size], part_total[:, lane + size : lane + 2 * size]
                    value = gate / (1.0 + jnp.exp(-gate)) * up * readout_ref[:, start : start + size]
                    if size % 128 == 0:
                        value = sum(value[:, k : k + 128] for k in range(0, size, 128))
                    line += jnp.sum(value.T, axis=0, keepdims=True)
                out = outs[own_out if mine else block_out]
                out[pl.ds(row, 1), :] += line

    results = pl.pallas_call(
        kernel,
        out_shape=shapes,
        in_specs=specs,
        out_specs=[pl.BlockSpec(memory_space=pltpu.VMEM)] * len(shapes),
        scratch_shapes=scratch,
        compiler_params=pltpu.CompilerParams(vmem_limit_bytes=VMEM_BYTES),
        cost_estimate=SMALL,
    )(*arrays)
    return (results[own_out] if used_tiles else None), (results[block_out] if used_blocks else None)


def noise_columns(gate, up, cuts):
    blocks = []
    for begin, size in cuts:
        blocks += [gate[:, begin : begin + size], up[:, begin : begin + size]]
    value = jnp.concatenate(blocks, 1).astype(BF16)
    return jnp.concatenate([value] * 3, 0)


def lanes_from(ref, start, width, row=None):
    if start is None:
        return ref[...] if row is None else ref[row]
    lanes = pl.ds(pl.multiple_of(start * 128, 128), width)
    return ref[:, lanes] if row is None else ref[row, :, lanes]


def own_factors(starts, tokens, a_gate, a_up, gate_cols, up_cols, gate_half, up_half, fitness, scale, cuts, waited):
    members, tok_count, width = tokens.shape
    rank, hidden = a_gate.shape[1], gate_cols.shape[2]
    half, lines, block_half = hidden // 2, 2 * members * rank, width // 2
    halves = [] if gate_half is None else [gate_half, up_half]

    def kernel(starts_ref, tok_ref, ag, au, gc, uc, fit, waited_ref, *refs):
        bundle, rows, cols = refs[-3:]

        def both(gate, up):
            found = []
            for m in range(members):
                found += [gate(m).astype(F32), up(m).astype(F32)]
            return jnp.concatenate(found, 0).astype(BF16)

        bundle[:, :hidden] = both(lambda m: gc[m], lambda m: uc[m])
        bundle[:, hidden : hidden + block_half] = both(
            lambda m: lanes_from(ag, starts_ref[0], block_half, m), lambda m: lanes_from(au, starts_ref[0], block_half, m)
        )
        marks = [jnp.broadcast_to(fit[:, m : m + 1].astype(F32), (2 * rank, 128)) for m in range(members)]
        bundle[:, hidden + block_half : hidden + block_half + 128] = jnp.concatenate(marks, 0).astype(BF16)
        terms = []
        for m in range(members):
            factors = jnp.concatenate([ag[m].astype(F32), au[m].astype(F32)], 0).astype(BF16)
            value = scale * lax.dot_general(
                factors, tok_ref[m], (((1,), (1,)), ((), ())), preferred_element_type=F32
            )
            found = []
            for _ in range(3):
                found.append(value.astype(BF16).astype(F32))
                value = value - found[-1]
            terms.append(found)
            zero = jnp.zeros_like(value)
            lines_of = [found[n] if other == m else zero for n in range(3) for other in range(members)]
            rows[m] = jnp.concatenate(lines_of, 0).astype(BF16)
        ends = jnp.concatenate([jnp.concatenate(found, 1) for found in terms], 0)
        bundle[:, hidden + block_half + 128 :] = ends.astype(BF16)
        gates, ups = [], []
        for m in range(members):
            if halves:
                gate, up = refs[0][m].astype(F32), refs[1][m].astype(F32)
            else:
                gate = lanes_from(gc, starts_ref[1], half, m).astype(F32)
                up = lanes_from(uc, starts_ref[1], half, m).astype(F32)
            gates += [gate, jnp.zeros_like(gate)]
            ups += [jnp.zeros_like(up), up]
        cols[...] = noise_columns(jnp.concatenate(gates, 0), jnp.concatenate(ups, 0), cuts)

    vmem = pl.BlockSpec(memory_space=pltpu.VMEM)
    return pl.pallas_call(
        kernel,
        out_shape=[
            jax.ShapeDtypeStruct((lines, hidden + block_half + 128 + 3 * tok_count), BF16),
            jax.ShapeDtypeStruct((members, 3 * lines, tok_count), BF16),
            jax.ShapeDtypeStruct((3 * lines, 2 * half), BF16),
        ],
        in_specs=[pl.BlockSpec(memory_space=pltpu.SMEM)]
        + [vmem] * 6
        + [pl.BlockSpec(memory_space=pltpu.HBM)]
        + [vmem] * len(halves),
        out_specs=[vmem] * 3,
        compiler_params=pltpu.CompilerParams(vmem_limit_bytes=VMEM_BYTES),
        cost_estimate=SMALL,
    )(starts, tokens, a_gate, a_up, gate_cols, up_cols, fitness, waited, *halves)


def other_factors(starts, bundle, own_bundle, a_gate, a_up, half_cols, hidden, tok_count, tile, block_rows, cuts):
    members, rank, width = a_gate.shape
    lines, half, block_half = 2 * members * rank, hidden // 2, width // 2
    first = hidden + block_half + 128
    count, targets = members * tok_count // tile, (starts.shape[0] - 1) // 2
    halves = [] if half_cols is None else [half_cols]

    def kernel(starts_ref, bundle_ref, own_ref, ag, au, *refs):
        rows, cols = refs[len(halves) : len(halves) + 2]
        for block in range(count):
            m, at = block * tile // tok_count, block * tile % tok_count
            found = []
            for n in range(3):
                lane = first + n * tok_count + at
                value = bundle_ref[:, lane : lane + tile].astype(F32)
                line = lax.broadcasted_iota(jnp.int32, value.shape, 0)
                found.append(jnp.where(line // (2 * rank) == m, value, 0.0))
            rows[block] = jnp.concatenate(found, 0).astype(BF16)
        value = (refs[0][...] if halves else lanes_from(bundle_ref, starts_ref[0], half)).astype(F32)
        is_gate = lax.broadcasted_iota(jnp.int32, value.shape, 0) % (2 * rank) < rank
        cols[...] = noise_columns(jnp.where(is_gate, value, 0.0), jnp.where(is_gate, 0.0, value), cuts)
        for target in range(targets):
            pack = refs[len(halves) + 2 + target]
            pack[:lines, :hidden] = own_ref[:, :hidden]
            pack[lines:, :hidden] = bundle_ref[:, :hidden]
            mine = []
            for m in range(members):
                for source in (ag, au):
                    mine.append(lanes_from(source, starts_ref[2 + 2 * target], block_rows, m).astype(F32))
            pack[:lines, hidden : hidden + block_rows] = jnp.concatenate(mine, 0).astype(BF16)
            pack[lines:, hidden : hidden + block_rows] = lanes_from(
                bundle_ref, hidden // 128 + starts_ref[1 + 2 * target], block_rows
            )
            pack[:lines, hidden + block_rows :] = own_ref[:, first - 128 : first]
            pack[lines:, hidden + block_rows :] = bundle_ref[:, first - 128 : first]

    vmem = pl.BlockSpec(memory_space=pltpu.VMEM)
    return pl.pallas_call(
        kernel,
        out_shape=[
            jax.ShapeDtypeStruct((count, 3 * lines, tile), BF16),
            jax.ShapeDtypeStruct((3 * lines, 2 * half), BF16),
        ]
        + [jax.ShapeDtypeStruct((2 * lines, hidden + block_rows + 128), BF16)] * targets,
        in_specs=[pl.BlockSpec(memory_space=pltpu.SMEM)] + [vmem] * (4 + len(halves)),
        out_specs=[vmem] * (2 + targets),
        compiler_params=pltpu.CompilerParams(vmem_limit_bytes=VMEM_BYTES),
        cost_estimate=SMALL,
    )(starts, bundle, own_bundle, a_gate, a_up, *halves)


def update_directions(packs, hidden, block_rows, rank, total):
    step = 128

    def kernel(*refs):
        gate_out, up_out = refs[len(packs) :]
        lanes = pl.ds(pl.multiple_of(hidden + pl.program_id(0) * step, 128), step)
        left, right = [], []
        for ref in refs[: len(packs)]:
            value = ref[:, lanes].astype(F32) * (ref[:, hidden + block_rows : hidden + block_rows + 1].astype(F32) / math.sqrt(total))
            for _ in range(3):
                term = value.astype(BF16)
                left.append(term)
                value = value - term.astype(F32)
            right += [ref[:, :hidden]] * 3
        left, right = jnp.concatenate(left, 0), jnp.concatenate(right, 0)
        is_gate = lax.broadcasted_iota(jnp.int32, left.shape, 0) % (2 * rank) < rank
        for out, mask in ((gate_out, is_gate), (up_out, jnp.logical_not(is_gate))):
            part = jnp.where(mask, left.astype(F32), 0.0).astype(BF16)
            out[...] = lax.dot_general(part, right, (((0,), (0,)), ((), ())), preferred_element_type=F32)

    return pl.pallas_call(
        kernel,
        grid=(block_rows // step,),
        out_shape=[jax.ShapeDtypeStruct((block_rows, hidden), F32)] * 2,
        in_specs=[pl.BlockSpec(pack.shape, lambda i: (0, 0)) for pack in packs],
        out_specs=[pl.BlockSpec((step, hidden), lambda i: (i, 0))] * 2,
        compiler_params=pltpu.CompilerParams(vmem_limit_bytes=VMEM_BYTES),
        cost_estimate=SMALL,
    )(*packs)


def cut_blocks(gate, up, shift, groups, waited):
    rows = gate.shape[0]
    widths = [2 * sum(size for _, size in group) for group in groups]
    count = sum(2 * len(group) for group in groups)

    def kernel(shift_ref, gate_ref, up_ref, waited_ref, *refs):
        blocks, held, sems = refs[: len(groups)], refs[len(groups) : -1], refs[-1]
        first, used = [], 0
        for n, group in enumerate(groups):
            first.append([])
            for begin, size in group:
                lanes = pl.ds(pl.multiple_of(shift_ref[0] * 128 + begin, 128), size)
                to = 2 * (begin - group[0][0])
                for kind, source in enumerate((gate_ref, up_ref)):
                    target = held[n].at[:, pl.ds(to + kind * size, size)]
                    first[n].append(pltpu.make_async_copy(source.at[:, lanes], target, sems.at[used]))
                    first[n][-1].start()
                    used += 1
        second = []
        for n in range(len(groups)):
            for copy in first[n]:
                copy.wait()
            second.append(pltpu.make_async_copy(held[n], blocks[n], sems.at[used + n]))
            second[n].start()
        for copy in second:
            copy.wait()

    anywhere = pl.BlockSpec(memory_space=pltpu.HBM)
    return pl.pallas_call(
        kernel,
        out_shape=[jax.ShapeDtypeStruct((rows, width), gate.dtype) for width in widths],
        in_specs=[pl.BlockSpec(memory_space=pltpu.SMEM), anywhere, anywhere, anywhere],
        out_specs=[anywhere] * len(groups),
        scratch_shapes=[pltpu.VMEM((rows, width), gate.dtype) for width in widths]
        + [pltpu.SemaphoreType.DMA((count + len(groups),))],
        compiler_params=pltpu.CompilerParams(vmem_limit_bytes=VMEM_BYTES),
        cost_estimate=SMALL,
    )(shift, gate, up, waited)


def body(
    pop_size,
    shard_size,
    tokens,
    gate_weight_matrix,
    w_up,
    a_gate,
    a_up,
    gate_hidden_factors,
    up_hidden_factors,
    fitness,
    readout,
):
    members, tok_count, model_width = tokens.shape
    rank = a_gate.shape[1]
    rows = members * tok_count
    block_rows, hidden = gate_weight_matrix.shape
    half = hidden // 2
    lo_size = pop_size // 2
    outer, inner = line_sizes(shard_size)
    noise_scale = 0.25 / math.sqrt(model_width * rank)
    pop, shard = lax.axis_index("pop"), lax.axis_index("shard")
    hi, lo = pop // lo_size, pop % lo_size
    flat = tokens.reshape(rows, model_width)
    crossing = column_chunks(half)
    chunks = [chunk for group in crossing for chunk in group]

    across_pairs = [(p, (p + lo_size) % pop_size) for p in range(pop_size)]

    def across(value):
        return lax.ppermute(value, "pop", across_pairs)

    def along(value, step):
        pairs = [(p, p // lo_size * lo_size + (p + step) % lo_size) for p in range(pop_size)]
        return lax.ppermute(value, "pop", pairs)

    def outer_permute(value, target):
        pairs = [(s, target(s // inner), s % inner) for s in range(shard_size)]
        return lax.ppermute(value, "shard", [(s, z * inner + y) for s, z, y in pairs if z is not None])

    def inner_permute(value, target):
        pairs = [(s, s // inner, target(s % inner)) for s in range(shard_size)]
        return lax.ppermute(value, "shard", [(s, z * inner + y) for s, z, y in pairs if y is not None])

    z, y = shard // inner, shard % inner
    size_z, size_y = rows // outer, model_width // inner
    block = lax.dynamic_slice(flat, (z * size_z, y * size_y), (size_z, size_y))
    sent = across(block)

    block_half = model_width // 2
    by_start = half % 128 == 0

    def in_half(value):
        return None if by_start else lax.dynamic_slice_in_dim(value, hi * half, half, value.ndim - 1)

    def numbers(*values):
        return jnp.stack([jnp.asarray(value, jnp.int32) for value in values])

    half_start = hi * (half // 128)
    bundle, own_lines, own_columns = own_factors(
        numbers((1 - hi) * (block_half // 128), half_start),
        tokens,
        a_gate,
        a_up,
        gate_hidden_factors,
        up_hidden_factors,
        in_half(gate_hidden_factors),
        in_half(up_hidden_factors),
        fitness[None, :],
        noise_scale,
        chunks,
        block,
    )
    other_bundle = across(bundle)

    def pick(which):
        if half % 128 == 0:
            return cut_blocks(gate_weight_matrix, w_up, numbers(which * (half // 128)), crossing, bundle)
        gate = lax.dynamic_slice_in_dim(gate_weight_matrix, which * half, half, 1)
        up = lax.dynamic_slice_in_dim(w_up, which * half, half, 1)
        return [
            jnp.concatenate([part[:, begin : begin + size] for begin, size in group for part in (gate, up)], 1)
            for group in crossing
        ]

    cut = pick(1 - hi)
    if half % 128 == 0:
        near = [(along(gate_weight_matrix, step), along(w_up, step)) for step in range(1, lo_size)]
        near = [(gate_weight_matrix, w_up)] + near
    else:
        kept = jnp.concatenate(pick(hi), 1)
        near = [kept] + [along(kept, step) for step in range(1, lo_size)]

    sent = after(sent, *cut, *jax.tree.leaves(near[1:]))

    starts = [half_start]
    for step in range(lo_size):
        target = (lo + step) % lo_size
        starts += [target * (block_rows // 128), hi * (block_half // 128) + target * (block_rows // 128)]
    far_lines, far_columns, *packs = other_factors(
        numbers(*starts),
        other_bundle,
        bundle,
        a_gate,
        a_up,
        in_half(other_bundle[:, :hidden]),
        hidden,
        tok_count,
        size_z,
        block_rows,
        chunks,
    )
    packs = packs[:1] + [along(pack, step) for step, pack in enumerate(packs[1:], 1)]
    directions = update_directions(packs, hidden, block_rows, rank, pop_size * members * rank)

    half_readout = lax.dynamic_slice_in_dim(readout, hi * half, half, 0)[None, :]
    own = (tokens, own_lines, own_columns)
    held_at = pop_size + 1
    part_at = held_at + outer
    ids = numbers(
        *[hi * lo_size + (lo + lo_size - step) % lo_size for step in range(lo_size)],
        *[(1 - hi) * lo_size + (lo + lo_size - step) % lo_size for step in range(lo_size)],
        half_start,
        *line_places(outer, z),
        *line_places(inner, y),
    )

    steps = line_steps(sent, outer, z, outer_permute)
    held, spread, far, chunk_list = [sent], [line_gather(sent, inner, y, inner_permute)], [], []
    end = len(chunks)
    passed = [across(after(cut[0], other_bundle))] + [None] * (len(crossing) - 1)
    own_total = other_total = 0.0
    done, barrier = [0] * outer, list(directions)

    def gather_next():
        next(steps)
        held.append(steps.send(lambda value: after(value, *barrier)))
        spread.append(line_gather(held[-1], inner, y, inner_permute))

    def bring(j):
        if passed[j] is None:
            passed[j] = across(after(cut[j], *(far[j - 2] if j > 1 else packs)))
        return passed[j]

    def score(parts):
        nonlocal own_total, other_total
        blocks = [
            (held_at + n, [(piece, part_at + k) for k, piece in enumerate(pieces)])
            for n, pieces in enumerate(spread)
        ]
        mine, theirs = gated_scores(
            ids, chunk_list, own, (blocks, far_lines, far_columns), parts, half_readout
        )
        own_total = own_total if mine is None else own_total + mine.reshape(-1)
        other_total = other_total if theirs is None else other_total + theirs.reshape(-1)
        return [value for value in (mine, theirs) if value is not None]

    for j, group in enumerate(crossing):
        block = bring(j)
        if len(held) < outer:
            recent = spread[-1][-1]
            gather_next()
            block = after(block, held[-1], recent)
        elif j:
            block = after(block, *barrier)
        far.append([block] + [along(block, step) for step in range(1, lo_size)])
        for begin, size in group:
            sources = []
            for n, kept_block in enumerate(near):
                if half % 128 == 0:
                    sources += [(value, begin, pop_size, k * size, size, n) for k, value in enumerate(kept_block)]
                else:
                    sources.append((kept_block, 2 * begin, None, 0, 2 * size, n))
            at = 2 * (begin - group[0][0])
            sources += [(value, at, None, 0, 2 * size, lo_size + n) for n, value in enumerate(far[j])]
            chunk_list.append((begin, size, sources))
        there = len(chunk_list)
        parts = [(True, t, t + 1, i, i + 1) for i in range(there - len(group), there) for t in range(members)]
        if j < len(crossing) - 1:
            ready = min(j + 1, outer - 1)
            old = [n for n in range(ready) if done[n] == there - 1]
            if old:
                parts.append((False, old[0], old[-1] + 1, there - 1, there))
            for n in range(ready):
                parts += [(False, n, n + 1, i, i + 1) for i in range(done[n], there) if n not in old]
                done[n] = there
            barrier = score(parts)
    while len(held) < outer:
        gather_next()
    rest = [(False, n, n + 1, i, i + 1) for n in range(outer) for i in range(done[n], end - 1)]
    score(rest + [(False, 0, outer, end - 1, end)] + parts)

    crossed = across(other_total)
    near_own = [inner_permute(own_total, lambda c, s=s: (c + s) % inner) for s in range(1, inner)]
    near_other = [
        lax.ppermute(
            other_total,
            ("pop", "shard"),
            [
                (p * shard_size + s, (p + lo_size) % pop_size * shard_size + s // inner * inner + (s + step) % inner)
                for p in range(pop_size)
                for s in range(shard_size)
            ],
        )
        for step in range(1, inner)
    ]
    scores = own_total + crossed + sum(near_own) + sum(near_other)
    scores = scores + sum(outer_permute(scores, lambda c, s=s: (c + s) % outer) for s in range(1, outer))
    return scores.reshape(members, tok_count), directions[0], directions[1]


def solution(mesh):
    placed = (
        P("pop", None, None),
        P("pop", "shard"),
        P("pop", "shard"),
        P("pop", None, None),
        P("pop", None, None),
        P("pop", None, "shard"),
        P("pop", None, "shard"),
        P("pop"),
        P("shard"),
    )
    return jax.shard_map(
        functools.partial(body, mesh.shape["pop"], mesh.shape["shard"]),
        mesh=mesh,
        in_specs=placed,
        out_specs=(P("pop", None), P("pop", "shard"), P("pop", "shard")),
        check_vma=False,
    )
```

```python
import functools
import math

import jax
import jax.numpy as jnp
from jax import lax
from jax.experimental import pallas as pl
from jax.experimental.pallas import tpu as pltpu
from jax.sharding import PartitionSpec as P

F32 = jnp.float32
BF16 = jnp.bfloat16
MIB = 1024 * 1024
VMEM_BYTES = 64 * MIB
SMALL = pl.CostEstimate(flops=1, bytes_accessed=1, transcendentals=0)


def split3(value):
    top = lax.reduce_precision(value, 8, 7)
    rest = value - top
    middle = lax.reduce_precision(rest, 8, 7)
    return [term.astype(BF16) for term in (top, middle, rest - middle)]


def column_chunks(width):
    groups, begin = [], 0
    while begin < width:
        end, group = min(begin + (384 if len(groups) == 1 else 256), width), []
        while begin < end:
            group.append((begin, min(256, end - begin)))
            begin += group[-1][1]
        groups.append(group)
    return groups


def line_sizes(total):
    outer = 4 if total % 4 == 0 else 1
    return outer, total // outer


def swap_pairs(total, partner):
    return [(index, partner(index)) for index in range(total)]


def line_steps(own, size, coord, permute):
    if size != 4:
        for step in range(1, size):
            block = permute(own, lambda c, step=step: (c + step) % size)
            hold = yield
            yield hold(block)
        return
    even = lambda c: c ^ 1
    odd = lambda c: 3 - c if c in (1, 2) else None
    edge = jnp.logical_or(coord == 0, coord == 3)
    first, across = permute(own, even), permute(own, odd)
    hold = yield
    first, across = hold(first), hold(across)
    yield first
    ahead, over = permute(across, even), permute(first, odd)
    hold = yield
    ahead, over = hold(ahead), hold(over)
    yield jnp.where(edge, ahead, across)
    ahead = permute(over, even)
    hold = yield
    yield jnp.where(edge, hold(ahead), over)


def line_places(size, coord):
    if size != 4:
        return [coord] + [(coord + size - step) % size for step in range(1, size)]
    return [coord] + [
        jnp.where(coord == 0, a, jnp.where(coord == 1, b, jnp.where(coord == 2, c, d)))
        for a, b, c, d in ((1, 0, 3, 2), (2, 2, 1, 1), (3, 3, 0, 0))
    ]


def line_gather(own, size, coord, permute):
    found, steps = [own], line_steps(own, size, coord, permute)
    for _ in range(size - 1):
        next(steps)
        found.append(steps.send(lambda value: value))
    return found


def after(value, *others):
    anywhere = pl.BlockSpec(memory_space=pltpu.HBM)
    return pl.pallas_call(
        lambda *refs: None,
        out_shape=jax.ShapeDtypeStruct(value.shape, value.dtype),
        in_specs=[anywhere] * (1 + len(others)),
        out_specs=anywhere,
        input_output_aliases={0: 0},
        compiler_params=pltpu.CompilerParams(vmem_limit_bytes=VMEM_BYTES),
        cost_estimate=SMALL,
    )(value, *others)


def gated_scores(ids, chunks, own, blocks, parts, readout, carried):
    arrays, specs, scratch, shapes, copies = [], [], [], [], 0

    def add(array, space):
        for index, seen in enumerate(arrays):
            if seen is array:
                return index
        arrays.append(array)
        specs.append(pl.BlockSpec(memory_space=space))
        return len(arrays) - 1

    add(ids, pltpu.SMEM)
    small = []

    def add_small(array):
        small.append((add(array, pltpu.HBM), len(scratch)))
        scratch.append(pltpu.VMEM(array.shape, array.dtype))
        return small[-1][1]

    lines = own[1].shape[1]
    tiles, tile, width = own[0].shape
    place_count, block_rows = blocks[1].shape[0], blocks[1].shape[2]
    chunk_rows = chunks[0][2][0][0].shape[0]
    used_chunks = sorted({j for part in parts for j in range(part[3], part[4])})
    used_tiles = sorted({t for part in parts if part[0] for t in range(part[1], part[2])})
    used_blocks = sorted({t for part in parts if not part[0] for t in range(part[1], part[2])})
    lane_at, total_lanes = {}, 0
    for j in used_chunks:
        lane_at[j] = total_lanes
        total_lanes += 2 * chunks[j][1]
    weights_at = len(scratch)
    scratch.append(pltpu.VMEM((width, total_lanes), BF16))
    chunk_refs = {j: [(add(source[0], pltpu.HBM),) + source[1:] for source in chunks[j][2]] for j in used_chunks}
    copies += sum(len(refs) for refs in chunk_refs.values())
    own_at = block_at = own_out = block_out = None
    if used_tiles:
        own_at, own_out = len(scratch), len(shapes)
        scratch.append(pltpu.VMEM((len(used_tiles) * tile, width), BF16))
        shapes.append(jax.ShapeDtypeStruct((place_count, block_rows), F32))
        own_ref, own_lines, own_cols = add(own[0], pltpu.HBM), add_small(own[1]), add_small(own[2])
        copies += len(used_tiles)
    if used_blocks:
        block_at, block_out = len(scratch), len(shapes)
        scratch.append(pltpu.VMEM((len(used_blocks) * block_rows, width), BF16))
        shapes.append(jax.ShapeDtypeStruct((place_count, block_rows), F32))
        far_lines, far_cols = add_small(blocks[1]), add_small(blocks[2])
        block_refs = {n: [(add(array, pltpu.HBM), place) for array, place in blocks[0][n][1]] for n in used_blocks}
        copies += sum(len(refs) for refs in block_refs.values())
    readout_at = add_small(readout)
    carry = [
        (out, add_small(value)) for out, value in zip((own_out, block_out), carried) if out is not None and value is not None
    ]
    scratch.append(pltpu.SemaphoreType.DMA((copies + len(small),)))
    inputs, outputs = len(arrays), len(shapes)

    def kernel(*refs):
        ids_ref = refs[0]
        outs, held = refs[inputs : inputs + outputs], refs[inputs + outputs :]
        sems, readout_ref = held[-1], held[readout_at]
        pending, count = {}, 0

        def fetch(key):
            nonlocal count
            if key in pending:
                return
            pairs = []
            if key[0] == "chunk":
                for index, lane, shift, to, lanes, place in chunk_refs[key[1]]:
                    first = pl.multiple_of(ids_ref[place] * chunk_rows, chunk_rows)
                    if shift is not None:
                        lane = pl.multiple_of(ids_ref[shift] * 128 + lane, 128)
                    source = refs[index].at[:, pl.ds(lane, lanes)]
                    target = held[weights_at].at[pl.ds(first, chunk_rows), pl.ds(lane_at[key[1]] + to, lanes)]
                    pairs.append((source, target))
            elif key[0] == "own":
                rows = pl.ds(used_tiles.index(key[1]) * tile, tile)
                pairs.append((refs[own_ref].at[key[1]], held[own_at].at[rows, :]))
            else:
                for index, place in block_refs[key[1]]:
                    lanes = refs[index].shape[1]
                    first = pl.multiple_of(ids_ref[place] * lanes, lanes)
                    rows = pl.ds(used_blocks.index(key[1]) * block_rows, block_rows)
                    target = held[block_at].at[rows, pl.ds(first, lanes)]
                    pairs.append((refs[index], target))
            pending[key] = []
            for source, target in pairs:
                pending[key].append(pltpu.make_async_copy(source, target, sems.at[count]))
                pending[key][-1].start()
                count += 1

        def keys(part):
            mine, begin, end, first, last = part
            found = [("chunk", j) for j in range(first, last)]
            return found + [("own" if mine else "block", n) for n in range(begin, end)]

        first_copies = []
        for n, (index, place) in enumerate(small):
            first_copies.append(pltpu.make_async_copy(refs[index], held[place], sems.at[copies + n]))
            first_copies[-1].start()
        for part in parts[:2]:
            for key in keys(part):
                fetch(key)
        for n, out in enumerate(outs):
            if n not in dict(carry):
                out[...] = jnp.zeros(out.shape, F32)
        for copy in first_copies:
            copy.wait()
        for out, place in carry:
            outs[out][...] = held[place][...]
        for number, part in enumerate(parts):
            for key in keys(part):
                for copy in pending[key]:
                    copy.wait()
                pending[key] = []
            if number + 2 < len(parts):
                for key in keys(parts[number + 2]):
                    fetch(key)
            mine, begin, end, first, last = part
            if mine:
                held_rows, height, at = held[own_at], tile, used_tiles.index(begin)
            else:
                held_rows, height, at = held[block_at], block_rows, used_blocks.index(begin)
            lanes = slice(lane_at[first], lane_at[last - 1] + 2 * chunks[last - 1][1])
            top, tall = at * height, (end - begin) * height
            piece = 240 if lanes.stop - lanes.start <= 256 and tall % 240 == 0 else tall
            pieces = [
                jnp.dot(held_rows[top + k : top + k + piece, :], held[weights_at][:, lanes], preferred_element_type=F32)
                for k in range(0, tall, piece)
            ]
            total = jnp.concatenate(pieces, 0) if len(pieces) > 1 else pieces[0]
            for t in range(end - begin):
                if mine:
                    row, noise, columns = begin + t, held[own_lines].at[begin + t], held[own_cols]
                else:
                    row = ids_ref[blocks[0][begin + t][0]]
                    noise, columns = held[far_lines].at[row], held[far_cols]
                begin_lane = 2 * chunks[first][0]
                part_total = total[t * height : (t + 1) * height, :] + lax.dot_general(
                    noise[...],
                    columns[:, begin_lane : begin_lane + lanes.stop - lanes.start],
                    (((0,), (0,)), ((), ())),
                    preferred_element_type=F32,
                )
                line = 0.0
                for j in range(first, last):
                    start, size, _ = chunks[j]
                    lane = lane_at[j] - lane_at[first]
                    gate, up = part_total[:, lane : lane + size], part_total[:, lane + size : lane + 2 * size]
                    value = gate / (1.0 + jnp.exp(-gate)) * up * readout_ref[:, start : start + size]
                    if size % 128 == 0:
                        value = sum(value[:, k : k + 128] for k in range(0, size, 128))
                    line += jnp.sum(value.T, axis=0, keepdims=True)
                if mine:
                    for k in range(tile // block_rows):
                        at_row = row * (tile // block_rows) + k
                        outs[own_out][at_row : at_row + 1, :] += line[:, k * block_rows : (k + 1) * block_rows]
                else:
                    outs[block_out][pl.ds(row, 1), :] += line

    results = pl.pallas_call(
        kernel,
        out_shape=shapes,
        in_specs=specs,
        out_specs=[pl.BlockSpec(memory_space=pltpu.VMEM)] * len(shapes),
        scratch_shapes=scratch,
        compiler_params=pltpu.CompilerParams(vmem_limit_bytes=VMEM_BYTES),
        cost_estimate=SMALL,
    )(*arrays)
    return (results[own_out] if used_tiles else carried[0]), (results[block_out] if used_blocks else carried[1])


def noise_columns(gate, up, cuts):
    blocks = []
    for begin, size in cuts:
        blocks += [gate[:, begin : begin + size], up[:, begin : begin + size]]
    value = jnp.concatenate(blocks, 1).astype(BF16)
    return jnp.concatenate([value] * 3, 0)


def lanes_from(ref, start, width, row=None):
    if start is None:
        return ref[...] if row is None else ref[row]
    lanes = pl.ds(pl.multiple_of(start * 128, 128), width)
    return ref[:, lanes] if row is None else ref[row, :, lanes]


def own_factors(starts, tokens, a_gate, a_up, gate_cols, up_cols, gate_half, up_half, fitness, scale, cuts, waited):
    members, tok_count, width = tokens.shape
    rank, hidden = a_gate.shape[1], gate_cols.shape[2]
    half, lines, block_half = hidden // 2, 2 * members * rank, width // 2
    halves = [] if gate_half is None else [gate_half, up_half]

    def kernel(starts_ref, tok_ref, ag, au, gc, uc, fit, waited_ref, *refs):
        bundle, rows, cols = refs[-3:]

        def both(gate, up):
            found = []
            for m in range(members):
                found += [gate(m).astype(F32), up(m).astype(F32)]
            return jnp.concatenate(found, 0).astype(BF16)

        bundle[:, :hidden] = both(lambda m: gc[m], lambda m: uc[m])
        bundle[:, hidden : hidden + block_half] = both(
            lambda m: lanes_from(ag, starts_ref[0], block_half, m), lambda m: lanes_from(au, starts_ref[0], block_half, m)
        )
        marks = [jnp.broadcast_to(fit[:, m : m + 1].astype(F32), (2 * rank, 128)) for m in range(members)]
        bundle[:, hidden + block_half : hidden + block_half + 128] = jnp.concatenate(marks, 0).astype(BF16)
        terms = []
        for m in range(members):
            factors = jnp.concatenate([ag[m].astype(F32), au[m].astype(F32)], 0).astype(BF16)
            value = scale * lax.dot_general(
                factors, tok_ref[m], (((1,), (1,)), ((), ())), preferred_element_type=F32
            )
            found = []
            for _ in range(3):
                found.append(value.astype(BF16).astype(F32))
                value = value - found[-1]
            terms.append(found)
            zero = jnp.zeros_like(value)
            lines_of = [found[n] if other == m else zero for n in range(3) for other in range(members)]
            rows[m] = jnp.concatenate(lines_of, 0).astype(BF16)
        ends = jnp.concatenate([jnp.concatenate(found, 1) for found in terms], 0)
        bundle[:, hidden + block_half + 128 :] = ends.astype(BF16)
        gates, ups = [], []
        for m in range(members):
            if halves:
                gate, up = refs[0][m].astype(F32), refs[1][m].astype(F32)
            else:
                gate = lanes_from(gc, starts_ref[1], half, m).astype(F32)
                up = lanes_from(uc, starts_ref[1], half, m).astype(F32)
            gates += [gate, jnp.zeros_like(gate)]
            ups += [jnp.zeros_like(up), up]
        cols[...] = noise_columns(jnp.concatenate(gates, 0), jnp.concatenate(ups, 0), cuts)

    vmem = pl.BlockSpec(memory_space=pltpu.VMEM)
    return pl.pallas_call(
        kernel,
        out_shape=[
            jax.ShapeDtypeStruct((lines, hidden + block_half + 128 + 3 * tok_count), BF16),
            jax.ShapeDtypeStruct((members, 3 * lines, tok_count), BF16),
            jax.ShapeDtypeStruct((3 * lines, 2 * half), BF16),
        ],
        in_specs=[pl.BlockSpec(memory_space=pltpu.SMEM)]
        + [vmem] * 6
        + [pl.BlockSpec(memory_space=pltpu.HBM)]
        + [vmem] * len(halves),
        out_specs=[vmem] * 3,
        compiler_params=pltpu.CompilerParams(vmem_limit_bytes=VMEM_BYTES),
        cost_estimate=SMALL,
    )(starts, tokens, a_gate, a_up, gate_cols, up_cols, fitness, waited, *halves)


def other_factors(starts, bundle, own_bundle, a_gate, a_up, half_cols, hidden, tok_count, tile, block_rows, cuts):
    members, rank, width = a_gate.shape
    lines, half, block_half = 2 * members * rank, hidden // 2, width // 2
    first = hidden + block_half + 128
    count, targets = members * tok_count // tile, (starts.shape[0] - 1) // 2
    halves = [] if half_cols is None else [half_cols]

    def kernel(starts_ref, bundle_ref, own_ref, ag, au, *refs):
        rows, cols = refs[len(halves) : len(halves) + 2]
        for block in range(count):
            m, at = block * tile // tok_count, block * tile % tok_count
            found = []
            for n in range(3):
                lane = first + n * tok_count + at
                value = bundle_ref[:, lane : lane + tile].astype(F32)
                line = lax.broadcasted_iota(jnp.int32, value.shape, 0)
                found.append(jnp.where(line // (2 * rank) == m, value, 0.0))
            rows[block] = jnp.concatenate(found, 0).astype(BF16)
        value = (refs[0][...] if halves else lanes_from(bundle_ref, starts_ref[0], half)).astype(F32)
        is_gate = lax.broadcasted_iota(jnp.int32, value.shape, 0) % (2 * rank) < rank
        cols[...] = noise_columns(jnp.where(is_gate, value, 0.0), jnp.where(is_gate, 0.0, value), cuts)
        for target in range(targets):
            pack = refs[len(halves) + 2 + target]
            pack[:lines, :hidden] = own_ref[:, :hidden]
            pack[lines:, :hidden] = bundle_ref[:, :hidden]
            mine = []
            for m in range(members):
                for source in (ag, au):
                    mine.append(lanes_from(source, starts_ref[2 + 2 * target], block_rows, m).astype(F32))
            pack[:lines, hidden : hidden + block_rows] = jnp.concatenate(mine, 0).astype(BF16)
            pack[lines:, hidden : hidden + block_rows] = lanes_from(
                bundle_ref, hidden // 128 + starts_ref[1 + 2 * target], block_rows
            )
            pack[:lines, hidden + block_rows :] = own_ref[:, first - 128 : first]
            pack[lines:, hidden + block_rows :] = bundle_ref[:, first - 128 : first]

    vmem = pl.BlockSpec(memory_space=pltpu.VMEM)
    return pl.pallas_call(
        kernel,
        out_shape=[
            jax.ShapeDtypeStruct((count, 3 * lines, tile), BF16),
            jax.ShapeDtypeStruct((3 * lines, 2 * half), BF16),
        ]
        + [jax.ShapeDtypeStruct((2 * lines, hidden + block_rows + 128), BF16)] * targets,
        in_specs=[pl.BlockSpec(memory_space=pltpu.SMEM)] + [vmem] * (4 + len(halves)),
        out_specs=[vmem] * (2 + targets),
        compiler_params=pltpu.CompilerParams(vmem_limit_bytes=VMEM_BYTES),
        cost_estimate=SMALL,
    )(starts, bundle, own_bundle, a_gate, a_up, *halves)


def update_directions(packs, hidden, block_rows, rank, total):
    step = 128

    def kernel(*refs):
        gate_out, up_out = refs[len(packs) :]
        lanes = pl.ds(pl.multiple_of(hidden + pl.program_id(0) * step, 128), step)
        left, right = [], []
        for ref in refs[: len(packs)]:
            value = ref[:, lanes].astype(F32) * (ref[:, hidden + block_rows : hidden + block_rows + 1].astype(F32) / math.sqrt(total))
            for _ in range(3):
                term = value.astype(BF16)
                left.append(term)
                value = value - term.astype(F32)
            right += [ref[:, :hidden]] * 3
        left, right = jnp.concatenate(left, 0), jnp.concatenate(right, 0)
        is_gate = lax.broadcasted_iota(jnp.int32, left.shape, 0) % (2 * rank) < rank
        for out, mask in ((gate_out, is_gate), (up_out, jnp.logical_not(is_gate))):
            part = jnp.where(mask, left.astype(F32), 0.0).astype(BF16)
            out[...] = lax.dot_general(part, right, (((0,), (0,)), ((), ())), preferred_element_type=F32)

    return pl.pallas_call(
        kernel,
        grid=(block_rows // step,),
        out_shape=[jax.ShapeDtypeStruct((block_rows, hidden), F32)] * 2,
        in_specs=[pl.BlockSpec(pack.shape, lambda i: (0, 0)) for pack in packs],
        out_specs=[pl.BlockSpec((step, hidden), lambda i: (i, 0))] * 2,
        compiler_params=pltpu.CompilerParams(vmem_limit_bytes=VMEM_BYTES),
        cost_estimate=SMALL,
    )(*packs)


def cut_blocks(gate, up, shift, groups, waited):
    rows = gate.shape[0]
    widths = [2 * sum(size for _, size in group) for group in groups]
    count = sum(2 * len(group) for group in groups)

    def kernel(shift_ref, gate_ref, up_ref, waited_ref, *refs):
        blocks, held, sems = refs[: len(groups)], refs[len(groups) : -1], refs[-1]
        first, used = [], 0
        for n, group in enumerate(groups):
            first.append([])
            for begin, size in group:
                lanes = pl.ds(pl.multiple_of(shift_ref[0] * 128 + begin, 128), size)
                to = 2 * (begin - group[0][0])
                for kind, source in enumerate((gate_ref, up_ref)):
                    target = held[n].at[:, pl.ds(to + kind * size, size)]
                    first[n].append(pltpu.make_async_copy(source.at[:, lanes], target, sems.at[used]))
                    first[n][-1].start()
                    used += 1
        second = []
        for n in range(len(groups)):
            for copy in first[n]:
                copy.wait()
            second.append(pltpu.make_async_copy(held[n], blocks[n], sems.at[used + n]))
            second[n].start()
        for copy in second:
            copy.wait()

    anywhere = pl.BlockSpec(memory_space=pltpu.HBM)
    return pl.pallas_call(
        kernel,
        out_shape=[jax.ShapeDtypeStruct((rows, width), gate.dtype) for width in widths],
        in_specs=[pl.BlockSpec(memory_space=pltpu.SMEM), anywhere, anywhere, anywhere],
        out_specs=[anywhere] * len(groups),
        scratch_shapes=[pltpu.VMEM((rows, width), gate.dtype) for width in widths]
        + [pltpu.SemaphoreType.DMA((count + len(groups),))],
        compiler_params=pltpu.CompilerParams(vmem_limit_bytes=VMEM_BYTES),
        cost_estimate=SMALL,
    )(shift, gate, up, waited)


def body(
    pop_size,
    shard_size,
    tokens,
    gate_weight_matrix,
    w_up,
    a_gate,
    a_up,
    gate_hidden_factors,
    up_hidden_factors,
    fitness,
    readout,
):
    members, tok_count, model_width = tokens.shape
    rank = a_gate.shape[1]
    rows = members * tok_count
    block_rows, hidden = gate_weight_matrix.shape
    half = hidden // 2
    lo_size = pop_size // 2
    outer, inner = line_sizes(shard_size)
    noise_scale = 0.25 / math.sqrt(model_width * rank)
    pop, shard = lax.axis_index("pop"), lax.axis_index("shard")
    hi, lo = pop // lo_size, pop % lo_size
    flat = tokens.reshape(rows, model_width)
    crossing = column_chunks(half)
    chunks = [chunk for group in crossing for chunk in group]

    across_pairs = [(p, (p + lo_size) % pop_size) for p in range(pop_size)]

    def across(value):
        return lax.ppermute(value, "pop", across_pairs)

    def along(value, step):
        pairs = [(p, p // lo_size * lo_size + (p + step) % lo_size) for p in range(pop_size)]
        return lax.ppermute(value, "pop", pairs)

    def outer_permute(value, target):
        pairs = [(s, target(s // inner), s % inner) for s in range(shard_size)]
        return lax.ppermute(value, "shard", [(s, z * inner + y) for s, z, y in pairs if z is not None])

    def inner_permute(value, target):
        pairs = [(s, s // inner, target(s % inner)) for s in range(shard_size)]
        return lax.ppermute(value, "shard", [(s, z * inner + y) for s, z, y in pairs if y is not None])

    z, y = shard // inner, shard % inner
    size_z, size_y = rows // outer, model_width // inner
    block = lax.dynamic_slice(flat, (z * size_z, y * size_y), (size_z, size_y))
    sent = across(block)

    block_half = model_width // 2
    by_start = half % 128 == 0

    def in_half(value):
        return None if by_start else lax.dynamic_slice_in_dim(value, hi * half, half, value.ndim - 1)

    def numbers(*values):
        return jnp.stack([jnp.asarray(value, jnp.int32) for value in values])

    half_start = hi * (half // 128)
    bundle, own_lines, own_columns = own_factors(
        numbers((1 - hi) * (block_half // 128), half_start),
        tokens,
        a_gate,
        a_up,
        gate_hidden_factors,
        up_hidden_factors,
        in_half(gate_hidden_factors),
        in_half(up_hidden_factors),
        fitness[None, :],
        noise_scale,
        chunks,
        block,
    )
    other_bundle = across(bundle)

    def pick(which):
        if half % 128 == 0:
            return cut_blocks(gate_weight_matrix, w_up, numbers(which * (half // 128)), crossing, bundle)
        gate = lax.dynamic_slice_in_dim(gate_weight_matrix, which * half, half, 1)
        up = lax.dynamic_slice_in_dim(w_up, which * half, half, 1)
        return [
            jnp.concatenate([part[:, begin : begin + size] for begin, size in group for part in (gate, up)], 1)
            for group in crossing
        ]

    cut = pick(1 - hi)
    if half % 128 == 0:
        near = [(along(gate_weight_matrix, step), along(w_up, step)) for step in range(1, lo_size)]
        near = [(gate_weight_matrix, w_up)] + near
    else:
        kept = jnp.concatenate(pick(hi), 1)
        near = [kept] + [along(kept, step) for step in range(1, lo_size)]

    sent = after(sent, other_bundle, *cut, *jax.tree.leaves(near[1:]))

    starts = [half_start]
    for step in range(lo_size):
        target = (lo + step) % lo_size
        starts += [target * (block_rows // 128), hi * (block_half // 128) + target * (block_rows // 128)]
    far_lines, far_columns, *packs = other_factors(
        numbers(*starts),
        other_bundle,
        bundle,
        a_gate,
        a_up,
        in_half(other_bundle[:, :hidden]),
        hidden,
        tok_count,
        size_z,
        block_rows,
        chunks,
    )
    packs = packs[:1] + [along(pack, step) for step, pack in enumerate(packs[1:], 1)]
    directions = update_directions(packs, hidden, block_rows, rank, pop_size * members * rank)

    half_readout = lax.dynamic_slice_in_dim(readout, hi * half, half, 0)[None, :]
    own = (tokens, own_lines, own_columns)
    held_at = pop_size + 1
    part_at = held_at + outer
    ids = numbers(
        *[hi * lo_size + (lo + lo_size - step) % lo_size for step in range(lo_size)],
        *[(1 - hi) * lo_size + (lo + lo_size - step) % lo_size for step in range(lo_size)],
        half_start,
        *line_places(outer, z),
        *line_places(inner, y),
    )

    steps = line_steps(sent, outer, z, outer_permute)
    held, spread, far, chunk_list = [sent], [line_gather(sent, inner, y, inner_permute)], [], []
    end = len(chunks)
    passed = [across(cut[0])] + [None] * (len(crossing) - 1)
    own_total = other_total = None
    done, barrier = [0] * outer, list(directions)

    def gather_next():
        next(steps)
        held.append(steps.send(lambda value: after(value, *barrier) if barrier else value))
        spread.append(line_gather(held[-1], inner, y, inner_permute))

    def bring(j):
        if passed[j] is None:
            passed[j] = across(after(cut[j], *(far[j - 2] if j > 1 else packs)))
        return passed[j]

    def score(parts):
        nonlocal own_total, other_total
        blocks = [
            (held_at + n, [(piece, part_at + k) for k, piece in enumerate(pieces)])
            for n, pieces in enumerate(spread)
        ]
        mine, theirs = gated_scores(
            ids, chunk_list, own, (blocks, far_lines, far_columns), parts, half_readout, (own_total, other_total)
        )
        own_total, other_total = mine, theirs
        return [value for value in (mine, theirs) if value is not None]

    for j, group in enumerate(crossing):
        block = bring(j)
        if len(held) < outer:
            recent = spread[-1][-1]
            gather_next()
            block = after(block, held[-1], recent)
        elif j:
            block = after(block, *barrier)
        far.append([block] + [along(block, step) for step in range(1, lo_size)])
        for begin, size in group:
            sources = []
            for n, kept_block in enumerate(near):
                if half % 128 == 0:
                    sources += [(value, begin, pop_size, k * size, size, n) for k, value in enumerate(kept_block)]
                else:
                    sources.append((kept_block, 2 * begin, None, 0, 2 * size, n))
            at = 2 * (begin - group[0][0])
            sources += [(value, at, None, 0, 2 * size, lo_size + n) for n, value in enumerate(far[j])]
            chunk_list.append((begin, size, sources))
        there = len(chunk_list)
        parts = [(True, t, t + 1, i, i + 1) for i in range(there - len(group), there) for t in range(members)]
        ready = min(j + 1, outer - 1)
        old = [n for n in range(ready) if done[n] == there - len(group)]
        for i in range(there - len(group), there):
            if old:
                parts.append((False, old[0], old[-1] + 1, i, i + 1))
        for n in range(ready):
            parts += [(False, n, n + 1, i, i + 1) for i in range(done[n], there) if n not in old]
            done[n] = there
        barrier = score(parts)
    while len(held) < outer:
        gather_next()
    rest = []
    for n in range(outer):
        cuts_at = list(range(done[n], max(done[n], end - 2))) + [max(done[n], end - 2), end]
        rest += [(False, n, n + 1, a, b) for a, b in zip(cuts_at, cuts_at[1:]) if a < b]
    score(rest)

    crossed = across(other_total)
    near_own = [inner_permute(own_total, lambda c, s=s: (c + s) % inner) for s in range(1, inner)]
    near_other = [
        lax.ppermute(
            other_total,
            ("pop", "shard"),
            [
                (p * shard_size + s, (p + lo_size) % pop_size * shard_size + s // inner * inner + (s + step) % inner)
                for p in range(pop_size)
                for s in range(shard_size)
            ],
        )
        for step in range(1, inner)
    ]
    scores = own_total + crossed + sum(near_own) + sum(near_other)
    scores = scores + sum(outer_permute(scores, lambda c, s=s: (c + s) % outer) for s in range(1, outer))
    return scores.reshape(members, tok_count), directions[0], directions[1]


def solution(mesh):
    placed = (
        P("pop", None, None),
        P("pop", "shard"),
        P("pop", "shard"),
        P("pop", None, None),
        P("pop", None, None),
        P("pop", None, "shard"),
        P("pop", None, "shard"),
        P("pop"),
        P("shard"),
    )
    return jax.shard_map(
        functools.partial(body, mesh.shape["pop"], mesh.shape["shard"]),
        mesh=mesh,
        in_specs=placed,
        out_specs=(P("pop", None), P("pop", "shard"), P("pop", "shard")),
        check_vma=False,
    )
```

```python
import functools
import math

import jax
import jax.numpy as jnp
from jax import lax
from jax.experimental import pallas as pl
from jax.experimental.pallas import tpu as pltpu
from jax.sharding import PartitionSpec as P

F32 = jnp.float32
BF16 = jnp.bfloat16
MIB = 1024 * 1024
VMEM_BYTES = 64 * MIB
SMALL = pl.CostEstimate(flops=1, bytes_accessed=1, transcendentals=0)


def split3(value):
    top = lax.reduce_precision(value, 8, 7)
    rest = value - top
    middle = lax.reduce_precision(rest, 8, 7)
    return [term.astype(BF16) for term in (top, middle, rest - middle)]


def column_chunks(width):
    groups, begin = [], 0
    while begin < width:
        end, group = min(begin + (384 if len(groups) == 1 else 256), width), []
        while begin < end:
            group.append((begin, min(256, end - begin)))
            begin += group[-1][1]
        groups.append(group)
    return groups


def line_sizes(total):
    outer = 4 if total % 4 == 0 else 1
    return outer, total // outer


def swap_pairs(total, partner):
    return [(index, partner(index)) for index in range(total)]


def line_steps(own, size, coord, permute):
    if size != 4:
        for step in range(1, size):
            block = permute(own, lambda c, step=step: (c + step) % size)
            hold = yield
            yield hold(block)
        return
    even = lambda c: c ^ 1
    odd = lambda c: 3 - c if c in (1, 2) else None
    edge = jnp.logical_or(coord == 0, coord == 3)
    first, across = permute(own, even), permute(own, odd)
    hold = yield
    first, across = hold(first), hold(across)
    yield first
    ahead, over = permute(across, even), permute(first, odd)
    hold = yield
    ahead, over = hold(ahead), hold(over)
    yield jnp.where(edge, ahead, across)
    ahead = permute(over, even)
    hold = yield
    yield jnp.where(edge, hold(ahead), over)


def line_places(size, coord):
    if size != 4:
        return [coord] + [(coord + size - step) % size for step in range(1, size)]
    return [coord] + [
        jnp.where(coord == 0, a, jnp.where(coord == 1, b, jnp.where(coord == 2, c, d)))
        for a, b, c, d in ((1, 0, 3, 2), (2, 2, 1, 1), (3, 3, 0, 0))
    ]


def line_gather(own, size, coord, permute):
    found, steps = [own], line_steps(own, size, coord, permute)
    for _ in range(size - 1):
        next(steps)
        found.append(steps.send(lambda value: value))
    return found


def after(value, *others):
    anywhere = pl.BlockSpec(memory_space=pltpu.HBM)
    return pl.pallas_call(
        lambda *refs: None,
        out_shape=jax.ShapeDtypeStruct(value.shape, value.dtype),
        in_specs=[anywhere] * (1 + len(others)),
        out_specs=anywhere,
        input_output_aliases={0: 0},
        compiler_params=pltpu.CompilerParams(vmem_limit_bytes=VMEM_BYTES),
        cost_estimate=SMALL,
    )(value, *others)


def gated_scores(ids, chunks, own, blocks, parts, readout, carried):
    arrays, specs, scratch, shapes, copies = [], [], [], [], 0

    def add(array, space):
        for index, seen in enumerate(arrays):
            if seen is array:
                return index
        arrays.append(array)
        specs.append(pl.BlockSpec(memory_space=space))
        return len(arrays) - 1

    add(ids, pltpu.SMEM)
    small = []

    def add_small(array):
        small.append((add(array, pltpu.HBM), len(scratch)))
        scratch.append(pltpu.VMEM(array.shape, array.dtype))
        return small[-1][1]

    lines = own[1].shape[1]
    tiles, tile, width = own[0].shape
    place_count, block_rows = blocks[1].shape[0], blocks[1].shape[2]
    chunk_rows = chunks[0][2][0][0].shape[0]
    used_chunks = sorted({j for part in parts for j in range(part[3], part[4])})
    used_tiles = sorted({t for part in parts if part[0] for t in range(part[1], part[2])})
    used_blocks = sorted({t for part in parts if not part[0] for t in range(part[1], part[2])})
    lane_at, total_lanes = {}, 0
    for j in used_chunks:
        lane_at[j] = total_lanes
        total_lanes += 2 * chunks[j][1]
    weights_at = len(scratch)
    scratch.append(pltpu.VMEM((width, total_lanes), BF16))
    chunk_refs = {j: [(add(source[0], pltpu.HBM),) + source[1:] for source in chunks[j][2]] for j in used_chunks}
    copies += sum(len(refs) for refs in chunk_refs.values())
    own_at = block_at = own_out = block_out = None
    if used_tiles:
        own_at, own_out = len(scratch), len(shapes)
        scratch.append(pltpu.VMEM((len(used_tiles) * tile, width), BF16))
        shapes.append(jax.ShapeDtypeStruct((place_count, block_rows), F32))
        own_ref, own_lines, own_cols = add(own[0], pltpu.HBM), add_small(own[1]), add_small(own[2])
        copies += len(used_tiles)
    if used_blocks:
        block_at, block_out = len(scratch), len(shapes)
        scratch.append(pltpu.VMEM((len(used_blocks) * block_rows, width), BF16))
        shapes.append(jax.ShapeDtypeStruct((place_count, block_rows), F32))
        far_lines, far_cols = add_small(blocks[1]), add_small(blocks[2])
        block_refs = {n: [(add(array, pltpu.HBM), place) for array, place in blocks[0][n][1]] for n in used_blocks}
        copies += sum(len(refs) for refs in block_refs.values())
    sums_at = {}
    for mine, used, height in ((True, used_tiles, tile), (False, used_blocks, block_rows)):
        if used:
            sums_at[mine] = len(scratch)
            scratch.append(pltpu.VMEM((len(used) * height, 128), F32))
    readout_at = add_small(readout)
    carry = [
        (out, add_small(value)) for out, value in zip((own_out, block_out), carried) if out is not None and value is not None
    ]
    scratch.append(pltpu.SemaphoreType.DMA((copies + len(small),)))
    inputs, outputs = len(arrays), len(shapes)

    def kernel(*refs):
        ids_ref = refs[0]
        outs, held = refs[inputs : inputs + outputs], refs[inputs + outputs :]
        sems, readout_ref = held[-1], held[readout_at]
        pending, count = {}, 0

        def fetch(key):
            nonlocal count
            if key in pending:
                return
            pairs = []
            if key[0] == "chunk":
                for index, lane, shift, to, lanes, place in chunk_refs[key[1]]:
                    first = pl.multiple_of(ids_ref[place] * chunk_rows, chunk_rows)
                    if shift is not None:
                        lane = pl.multiple_of(ids_ref[shift] * 128 + lane, 128)
                    source = refs[index].at[:, pl.ds(lane, lanes)]
                    target = held[weights_at].at[pl.ds(first, chunk_rows), pl.ds(lane_at[key[1]] + to, lanes)]
                    pairs.append((source, target))
            elif key[0] == "own":
                rows = pl.ds(used_tiles.index(key[1]) * tile, tile)
                pairs.append((refs[own_ref].at[key[1]], held[own_at].at[rows, :]))
            else:
                for index, place in block_refs[key[1]]:
                    lanes = refs[index].shape[1]
                    first = pl.multiple_of(ids_ref[place] * lanes, lanes)
                    rows = pl.ds(used_blocks.index(key[1]) * block_rows, block_rows)
                    target = held[block_at].at[rows, pl.ds(first, lanes)]
                    pairs.append((refs[index], target))
            pending[key] = []
            for source, target in pairs:
                pending[key].append(pltpu.make_async_copy(source, target, sems.at[count]))
                pending[key][-1].start()
                count += 1

        def keys(part):
            mine, begin, end, first, last = part
            found = [("chunk", j) for j in range(first, last)]
            return found + [("own" if mine else "block", n) for n in range(begin, end)]

        first_copies = []
        for n, (index, place) in enumerate(small):
            first_copies.append(pltpu.make_async_copy(refs[index], held[place], sems.at[copies + n]))
            first_copies[-1].start()
        for part in parts[:2]:
            for key in keys(part):
                fetch(key)
        for n, out in enumerate(outs):
            if n not in dict(carry):
                out[...] = jnp.zeros(out.shape, F32)
        for copy in first_copies:
            copy.wait()
        for out, place in carry:
            outs[out][...] = held[place][...]
        summed = set()

        def add_line(mine, row, line):
            if not mine:
                outs[block_out][pl.ds(row, 1), :] += line
                return
            for k in range(tile // block_rows):
                at_row = row * (tile // block_rows) + k
                outs[own_out][at_row : at_row + 1, :] += line[:, k * block_rows : (k + 1) * block_rows]

        for number, part in enumerate(parts):
            for key in keys(part):
                for copy in pending[key]:
                    copy.wait()
                pending[key] = []
            if number + 2 < len(parts):
                for key in keys(parts[number + 2]):
                    fetch(key)
            mine, begin, end, first, last = part
            if mine:
                held_rows, height, at = held[own_at], tile, used_tiles.index(begin)
            else:
                held_rows, height, at = held[block_at], block_rows, used_blocks.index(begin)
            lanes = slice(lane_at[first], lane_at[last - 1] + 2 * chunks[last - 1][1])
            top, tall = at * height, (end - begin) * height
            piece = 240 if lanes.stop - lanes.start <= 256 and tall % 240 == 0 else tall
            pieces = [
                jnp.dot(held_rows[top + k : top + k + piece, :], held[weights_at][:, lanes], preferred_element_type=F32)
                for k in range(0, tall, piece)
            ]
            total = jnp.concatenate(pieces, 0) if len(pieces) > 1 else pieces[0]
            for t in range(end - begin):
                if mine:
                    row, noise, columns = begin + t, held[own_lines].at[begin + t], held[own_cols]
                else:
                    row = ids_ref[blocks[0][begin + t][0]]
                    noise, columns = held[far_lines].at[row], held[far_cols]
                begin_lane = 2 * chunks[first][0]
                part_total = total[t * height : (t + 1) * height, :] + lax.dot_general(
                    noise[...],
                    columns[:, begin_lane : begin_lane + lanes.stop - lanes.start],
                    (((0,), (0,)), ((), ())),
                    preferred_element_type=F32,
                )
                folded, lone = None, None
                for j in range(first, last):
                    start, size, _ = chunks[j]
                    lane = lane_at[j] - lane_at[first]
                    gate, up = part_total[:, lane : lane + size], part_total[:, lane + size : lane + 2 * size]
                    value = gate / (1.0 + jnp.exp(-gate)) * up * readout_ref[:, start : start + size]
                    if size % 128 == 0:
                        for k in range(0, size, 128):
                            block = value[:, k : k + 128]
                            folded = block if folded is None else folded + block
                    else:
                        line = jnp.sum(value.T, axis=0, keepdims=True)
                        lone = line if lone is None else lone + line
                if folded is not None:
                    there = held[sums_at[mine]].at[(at + t) * height : (at + t + 1) * height, :]
                    key = (mine, begin + t)
                    there[...] = folded + there[...] if key in summed else folded
                    summed.add(key)
                if lone is not None:
                    add_line(mine, row, lone)
        for mine, n in sorted(summed):
            height, used = (tile, used_tiles) if mine else (block_rows, used_blocks)
            value = held[sums_at[mine]][used.index(n) * height : (used.index(n) + 1) * height, :]
            row = n if mine else ids_ref[blocks[0][n][0]]
            add_line(mine, row, jnp.sum(value.T, axis=0, keepdims=True))

    results = pl.pallas_call(
        kernel,
        out_shape=shapes,
        in_specs=specs,
        out_specs=[pl.BlockSpec(memory_space=pltpu.VMEM)] * len(shapes),
        scratch_shapes=scratch,
        compiler_params=pltpu.CompilerParams(vmem_limit_bytes=VMEM_BYTES),
        cost_estimate=SMALL,
    )(*arrays)
    return (results[own_out] if used_tiles else carried[0]), (results[block_out] if used_blocks else carried[1])


def noise_columns(gate, up, cuts):
    blocks = []
    for begin, size in cuts:
        blocks += [gate[:, begin : begin + size], up[:, begin : begin + size]]
    value = jnp.concatenate(blocks, 1).astype(BF16)
    return jnp.concatenate([value] * 3, 0)


def lanes_from(ref, start, width, row=None):
    if start is None:
        return ref[...] if row is None else ref[row]
    lanes = pl.ds(pl.multiple_of(start * 128, 128), width)
    return ref[:, lanes] if row is None else ref[row, :, lanes]


def own_factors(starts, tokens, a_gate, a_up, gate_cols, up_cols, gate_half, up_half, fitness, scale, cuts, waited):
    members, tok_count, width = tokens.shape
    rank, hidden = a_gate.shape[1], gate_cols.shape[2]
    half, lines, block_half = hidden // 2, 2 * members * rank, width // 2
    halves = [] if gate_half is None else [gate_half, up_half]

    def kernel(starts_ref, tok_ref, ag, au, gc, uc, fit, waited_ref, *refs):
        bundle, rows, cols = refs[-3:]

        def both(gate, up):
            found = []
            for m in range(members):
                found += [gate(m).astype(F32), up(m).astype(F32)]
            return jnp.concatenate(found, 0).astype(BF16)

        bundle[:, :hidden] = both(lambda m: gc[m], lambda m: uc[m])
        bundle[:, hidden : hidden + block_half] = both(
            lambda m: lanes_from(ag, starts_ref[0], block_half, m), lambda m: lanes_from(au, starts_ref[0], block_half, m)
        )
        marks = [jnp.broadcast_to(fit[:, m : m + 1].astype(F32), (2 * rank, 128)) for m in range(members)]
        bundle[:, hidden + block_half : hidden + block_half + 128] = jnp.concatenate(marks, 0).astype(BF16)
        terms = []
        for m in range(members):
            factors = jnp.concatenate([ag[m].astype(F32), au[m].astype(F32)], 0).astype(BF16)
            value = scale * lax.dot_general(
                factors, tok_ref[m], (((1,), (1,)), ((), ())), preferred_element_type=F32
            )
            found = []
            for _ in range(3):
                found.append(value.astype(BF16).astype(F32))
                value = value - found[-1]
            terms.append(found)
            zero = jnp.zeros_like(value)
            lines_of = [found[n] if other == m else zero for n in range(3) for other in range(members)]
            rows[m] = jnp.concatenate(lines_of, 0).astype(BF16)
        ends = jnp.concatenate([jnp.concatenate(found, 1) for found in terms], 0)
        bundle[:, hidden + block_half + 128 :] = ends.astype(BF16)
        gates, ups = [], []
        for m in range(members):
            if halves:
                gate, up = refs[0][m].astype(F32), refs[1][m].astype(F32)
            else:
                gate = lanes_from(gc, starts_ref[1], half, m).astype(F32)
                up = lanes_from(uc, starts_ref[1], half, m).astype(F32)
            gates += [gate, jnp.zeros_like(gate)]
            ups += [jnp.zeros_like(up), up]
        cols[...] = noise_columns(jnp.concatenate(gates, 0), jnp.concatenate(ups, 0), cuts)

    vmem = pl.BlockSpec(memory_space=pltpu.VMEM)
    return pl.pallas_call(
        kernel,
        out_shape=[
            jax.ShapeDtypeStruct((lines, hidden + block_half + 128 + 3 * tok_count), BF16),
            jax.ShapeDtypeStruct((members, 3 * lines, tok_count), BF16),
            jax.ShapeDtypeStruct((3 * lines, 2 * half), BF16),
        ],
        in_specs=[pl.BlockSpec(memory_space=pltpu.SMEM)]
        + [vmem] * 6
        + [pl.BlockSpec(memory_space=pltpu.HBM)]
        + [vmem] * len(halves),
        out_specs=[vmem] * 3,
        compiler_params=pltpu.CompilerParams(vmem_limit_bytes=VMEM_BYTES),
        cost_estimate=SMALL,
    )(starts, tokens, a_gate, a_up, gate_cols, up_cols, fitness, waited, *halves)


def other_factors(starts, bundle, own_bundle, a_gate, a_up, half_cols, hidden, tok_count, tile, block_rows, cuts):
    members, rank, width = a_gate.shape
    lines, half, block_half = 2 * members * rank, hidden // 2, width // 2
    first = hidden + block_half + 128
    count, targets = members * tok_count // tile, (starts.shape[0] - 1) // 2
    halves = [] if half_cols is None else [half_cols]

    def kernel(starts_ref, bundle_ref, own_ref, ag, au, *refs):
        rows, cols = refs[len(halves) : len(halves) + 2]
        for block in range(count):
            m, at = block * tile // tok_count, block * tile % tok_count
            found = []
            for n in range(3):
                lane = first + n * tok_count + at
                value = bundle_ref[:, lane : lane + tile].astype(F32)
                line = lax.broadcasted_iota(jnp.int32, value.shape, 0)
                found.append(jnp.where(line // (2 * rank) == m, value, 0.0))
            rows[block] = jnp.concatenate(found, 0).astype(BF16)
        value = (refs[0][...] if halves else lanes_from(bundle_ref, starts_ref[0], half)).astype(F32)
        is_gate = lax.broadcasted_iota(jnp.int32, value.shape, 0) % (2 * rank) < rank
        cols[...] = noise_columns(jnp.where(is_gate, value, 0.0), jnp.where(is_gate, 0.0, value), cuts)
        for target in range(targets):
            pack = refs[len(halves) + 2 + target]
            pack[:lines, :hidden] = own_ref[:, :hidden]
            pack[lines:, :hidden] = bundle_ref[:, :hidden]
            mine = []
            for m in range(members):
                for source in (ag, au):
                    mine.append(lanes_from(source, starts_ref[2 + 2 * target], block_rows, m).astype(F32))
            pack[:lines, hidden : hidden + block_rows] = jnp.concatenate(mine, 0).astype(BF16)
            pack[lines:, hidden : hidden + block_rows] = lanes_from(
                bundle_ref, hidden // 128 + starts_ref[1 + 2 * target], block_rows
            )
            pack[:lines, hidden + block_rows :] = own_ref[:, first - 128 : first]
            pack[lines:, hidden + block_rows :] = bundle_ref[:, first - 128 : first]

    vmem = pl.BlockSpec(memory_space=pltpu.VMEM)
    return pl.pallas_call(
        kernel,
        out_shape=[
            jax.ShapeDtypeStruct((count, 3 * lines, tile), BF16),
            jax.ShapeDtypeStruct((3 * lines, 2 * half), BF16),
        ]
        + [jax.ShapeDtypeStruct((2 * lines, hidden + block_rows + 128), BF16)] * targets,
        in_specs=[pl.BlockSpec(memory_space=pltpu.SMEM)] + [vmem] * (4 + len(halves)),
        out_specs=[vmem] * (2 + targets),
        compiler_params=pltpu.CompilerParams(vmem_limit_bytes=VMEM_BYTES),
        cost_estimate=SMALL,
    )(starts, bundle, own_bundle, a_gate, a_up, *halves)


def update_directions(packs, hidden, block_rows, rank, total):
    step = 128

    def kernel(*refs):
        gate_out, up_out = refs[len(packs) :]
        lanes = pl.ds(pl.multiple_of(hidden + pl.program_id(0) * step, 128), step)
        left, right = [], []
        for ref in refs[: len(packs)]:
            value = ref[:, lanes].astype(F32) * (ref[:, hidden + block_rows : hidden + block_rows + 1].astype(F32) / math.sqrt(total))
            for _ in range(3):
                term = value.astype(BF16)
                left.append(term)
                value = value - term.astype(F32)
            right += [ref[:, :hidden]] * 3
        left, right = jnp.concatenate(left, 0), jnp.concatenate(right, 0)
        is_gate = lax.broadcasted_iota(jnp.int32, left.shape, 0) % (2 * rank) < rank
        for out, mask in ((gate_out, is_gate), (up_out, jnp.logical_not(is_gate))):
            part = jnp.where(mask, left.astype(F32), 0.0).astype(BF16)
            out[...] = lax.dot_general(part, right, (((0,), (0,)), ((), ())), preferred_element_type=F32)

    return pl.pallas_call(
        kernel,
        grid=(block_rows // step,),
        out_shape=[jax.ShapeDtypeStruct((block_rows, hidden), F32)] * 2,
        in_specs=[pl.BlockSpec(pack.shape, lambda i: (0, 0)) for pack in packs],
        out_specs=[pl.BlockSpec((step, hidden), lambda i: (i, 0))] * 2,
        compiler_params=pltpu.CompilerParams(vmem_limit_bytes=VMEM_BYTES),
        cost_estimate=SMALL,
    )(*packs)


def cut_blocks(gate, up, shift, groups, waited):
    rows = gate.shape[0]
    widths = [2 * sum(size for _, size in group) for group in groups]
    count = sum(2 * len(group) for group in groups)

    def kernel(shift_ref, gate_ref, up_ref, waited_ref, *refs):
        blocks, held, sems = refs[: len(groups)], refs[len(groups) : -1], refs[-1]
        first, used = [], 0
        for n, group in enumerate(groups):
            first.append([])
            for begin, size in group:
                lanes = pl.ds(pl.multiple_of(shift_ref[0] * 128 + begin, 128), size)
                to = 2 * (begin - group[0][0])
                for kind, source in enumerate((gate_ref, up_ref)):
                    target = held[n].at[:, pl.ds(to + kind * size, size)]
                    first[n].append(pltpu.make_async_copy(source.at[:, lanes], target, sems.at[used]))
                    first[n][-1].start()
                    used += 1
        second = []
        for n in range(len(groups)):
            for copy in first[n]:
                copy.wait()
            second.append(pltpu.make_async_copy(held[n], blocks[n], sems.at[used + n]))
            second[n].start()
        for copy in second:
            copy.wait()

    anywhere = pl.BlockSpec(memory_space=pltpu.HBM)
    return pl.pallas_call(
        kernel,
        out_shape=[jax.ShapeDtypeStruct((rows, width), gate.dtype) for width in widths],
        in_specs=[pl.BlockSpec(memory_space=pltpu.SMEM), anywhere, anywhere, anywhere],
        out_specs=[anywhere] * len(groups),
        scratch_shapes=[pltpu.VMEM((rows, width), gate.dtype) for width in widths]
        + [pltpu.SemaphoreType.DMA((count + len(groups),))],
        compiler_params=pltpu.CompilerParams(vmem_limit_bytes=VMEM_BYTES),
        cost_estimate=SMALL,
    )(shift, gate, up, waited)


def body(
    pop_size,
    shard_size,
    tokens,
    gate_weight_matrix,
    w_up,
    a_gate,
    a_up,
    gate_hidden_factors,
    up_hidden_factors,
    fitness,
    readout,
):
    members, tok_count, model_width = tokens.shape
    rank = a_gate.shape[1]
    rows = members * tok_count
    block_rows, hidden = gate_weight_matrix.shape
    half = hidden // 2
    lo_size = pop_size // 2
    outer, inner = line_sizes(shard_size)
    noise_scale = 0.25 / math.sqrt(model_width * rank)
    pop, shard = lax.axis_index("pop"), lax.axis_index("shard")
    hi, lo = pop // lo_size, pop % lo_size
    flat = tokens.reshape(rows, model_width)
    crossing = column_chunks(half)
    chunks = [chunk for group in crossing for chunk in group]

    across_pairs = [(p, (p + lo_size) % pop_size) for p in range(pop_size)]

    def across(value):
        return lax.ppermute(value, "pop", across_pairs)

    def along(value, step):
        pairs = [(p, p // lo_size * lo_size + (p + step) % lo_size) for p in range(pop_size)]
        return lax.ppermute(value, "pop", pairs)

    def outer_permute(value, target):
        pairs = [(s, target(s // inner), s % inner) for s in range(shard_size)]
        return lax.ppermute(value, "shard", [(s, z * inner + y) for s, z, y in pairs if z is not None])

    def inner_permute(value, target):
        pairs = [(s, s // inner, target(s % inner)) for s in range(shard_size)]
        return lax.ppermute(value, "shard", [(s, z * inner + y) for s, z, y in pairs if y is not None])

    z, y = shard // inner, shard % inner
    size_z, size_y = rows // outer, model_width // inner
    block = lax.dynamic_slice(flat, (z * size_z, y * size_y), (size_z, size_y))
    sent = across(block)

    block_half = model_width // 2
    by_start = half % 128 == 0

    def in_half(value):
        return None if by_start else lax.dynamic_slice_in_dim(value, hi * half, half, value.ndim - 1)

    def numbers(*values):
        return jnp.stack([jnp.asarray(value, jnp.int32) for value in values])

    half_start = hi * (half // 128)
    bundle, own_lines, own_columns = own_factors(
        numbers((1 - hi) * (block_half // 128), half_start),
        tokens,
        a_gate,
        a_up,
        gate_hidden_factors,
        up_hidden_factors,
        in_half(gate_hidden_factors),
        in_half(up_hidden_factors),
        fitness[None, :],
        noise_scale,
        chunks,
        block,
    )
    other_bundle = across(bundle)

    def pick(which):
        if half % 128 == 0:
            return cut_blocks(gate_weight_matrix, w_up, numbers(which * (half // 128)), crossing, bundle)
        gate = lax.dynamic_slice_in_dim(gate_weight_matrix, which * half, half, 1)
        up = lax.dynamic_slice_in_dim(w_up, which * half, half, 1)
        return [
            jnp.concatenate([part[:, begin : begin + size] for begin, size in group for part in (gate, up)], 1)
            for group in crossing
        ]

    cut = pick(1 - hi)
    if half % 128 == 0:
        near = [(along(gate_weight_matrix, step), along(w_up, step)) for step in range(1, lo_size)]
        near = [(gate_weight_matrix, w_up)] + near
    else:
        kept = jnp.concatenate(pick(hi), 1)
        near = [kept] + [along(kept, step) for step in range(1, lo_size)]

    sent = after(sent, other_bundle, *cut, *jax.tree.leaves(near[1:]))

    starts = [half_start]
    for step in range(lo_size):
        target = (lo + step) % lo_size
        starts += [target * (block_rows // 128), hi * (block_half // 128) + target * (block_rows // 128)]
    far_lines, far_columns, *packs = other_factors(
        numbers(*starts),
        other_bundle,
        bundle,
        a_gate,
        a_up,
        in_half(other_bundle[:, :hidden]),
        hidden,
        tok_count,
        size_z,
        block_rows,
        chunks,
    )
    packs = packs[:1] + [along(pack, step) for step, pack in enumerate(packs[1:], 1)]
    directions = update_directions(packs, hidden, block_rows, rank, pop_size * members * rank)

    half_readout = lax.dynamic_slice_in_dim(readout, hi * half, half, 0)[None, :]
    own = (tokens, own_lines, own_columns)
    held_at = pop_size + 1
    part_at = held_at + outer
    ids = numbers(
        *[hi * lo_size + (lo + lo_size - step) % lo_size for step in range(lo_size)],
        *[(1 - hi) * lo_size + (lo + lo_size - step) % lo_size for step in range(lo_size)],
        half_start,
        *line_places(outer, z),
        *line_places(inner, y),
    )

    steps = line_steps(sent, outer, z, outer_permute)
    held, spread, far, chunk_list = [sent], [line_gather(sent, inner, y, inner_permute)], [], []
    end = len(chunks)
    passed = [across(cut[0])] + [None] * (len(crossing) - 1)
    own_total = other_total = None
    done, barrier = [0] * outer, list(directions)

    def gather_next():
        next(steps)
        held.append(steps.send(lambda value: after(value, *barrier) if barrier else value))
        spread.append(line_gather(held[-1], inner, y, inner_permute))

    def bring(j):
        if passed[j] is None:
            passed[j] = across(after(cut[j], *(far[j - 2] if j > 1 else packs)))
        return passed[j]

    def score(parts):
        nonlocal own_total, other_total
        blocks = [
            (held_at + n, [(piece, part_at + k) for k, piece in enumerate(pieces)])
            for n, pieces in enumerate(spread)
        ]
        mine, theirs = gated_scores(
            ids, chunk_list, own, (blocks, far_lines, far_columns), parts, half_readout, (own_total, other_total)
        )
        own_total, other_total = mine, theirs
        return [value for value in (mine, theirs) if value is not None]

    for j, group in enumerate(crossing):
        block = bring(j)
        if len(held) < outer:
            recent = spread[-1][-1]
            gather_next()
            block = after(block, held[-1], recent)
        elif j:
            block = after(block, *barrier)
        far.append([block] + [along(block, step) for step in range(1, lo_size)])
        for begin, size in group:
            sources = []
            for n, kept_block in enumerate(near):
                if half % 128 == 0:
                    sources += [(value, begin, pop_size, k * size, size, n) for k, value in enumerate(kept_block)]
                else:
                    sources.append((kept_block, 2 * begin, None, 0, 2 * size, n))
            at = 2 * (begin - group[0][0])
            sources += [(value, at, None, 0, 2 * size, lo_size + n) for n, value in enumerate(far[j])]
            chunk_list.append((begin, size, sources))
        there = len(chunk_list)
        parts = [(True, t, t + 1, i, i + 1) for i in range(there - len(group), there) for t in range(members)]
        ready = min(j + 1, outer - 1)
        old = [n for n in range(ready) if done[n] == there - len(group)]
        for i in range(there - len(group), there):
            if old:
                parts.append((False, old[0], old[-1] + 1, i, i + 1))
        for n in range(ready):
            parts += [(False, n, n + 1, i, i + 1) for i in range(done[n], there) if n not in old]
            done[n] = there
        barrier = score(parts)
    while len(held) < outer:
        gather_next()
    rest = []
    for n in range(outer):
        cuts_at = list(range(done[n], max(done[n], end - 2))) + [max(done[n], end - 2), end]
        rest += [(False, n, n + 1, a, b) for a, b in zip(cuts_at, cuts_at[1:]) if a < b]
    score(rest)

    crossed = across(other_total)
    near_own = [inner_permute(own_total, lambda c, s=s: (c + s) % inner) for s in range(1, inner)]
    near_other = [
        lax.ppermute(
            other_total,
            ("pop", "shard"),
            [
                (p * shard_size + s, (p + lo_size) % pop_size * shard_size + s // inner * inner + (s + step) % inner)
                for p in range(pop_size)
                for s in range(shard_size)
            ],
        )
        for step in range(1, inner)
    ]
    scores = own_total + crossed + sum(near_own) + sum(near_other)
    scores = scores + sum(outer_permute(scores, lambda c, s=s: (c + s) % outer) for s in range(1, outer))
    return scores.reshape(members, tok_count), directions[0], directions[1]


def solution(mesh):
    placed = (
        P("pop", None, None),
        P("pop", "shard"),
        P("pop", "shard"),
        P("pop", None, None),
        P("pop", None, None),
        P("pop", None, "shard"),
        P("pop", None, "shard"),
        P("pop"),
        P("shard"),
    )
    return jax.shard_map(
        functools.partial(body, mesh.shape["pop"], mesh.shape["shard"]),
        mesh=mesh,
        in_specs=placed,
        out_specs=(P("pop", None), P("pop", "shard"), P("pop", "shard")),
        check_vma=False,
    )
```

```python
import functools
import math

import jax
import jax.numpy as jnp
from jax import lax
from jax.experimental import pallas as pl
from jax.experimental.pallas import tpu as pltpu
from jax.sharding import PartitionSpec as P

F32 = jnp.float32
BF16 = jnp.bfloat16
MIB = 1024 * 1024
VMEM_BYTES = 64 * MIB
SMALL = pl.CostEstimate(flops=1, bytes_accessed=1, transcendentals=0)


def split3(value):
    top = lax.reduce_precision(value, 8, 7)
    rest = value - top
    middle = lax.reduce_precision(rest, 8, 7)
    return [term.astype(BF16) for term in (top, middle, rest - middle)]


def column_chunks(width):
    groups, begin = [], 0
    while begin < width:
        end, group = min(begin + (384 if len(groups) == 1 else 256), width), []
        while begin < end:
            group.append((begin, min(256, end - begin)))
            begin += group[-1][1]
        groups.append(group)
    return groups


def line_sizes(total):
    outer = 4 if total % 4 == 0 else 1
    return outer, total // outer


def swap_pairs(total, partner):
    return [(index, partner(index)) for index in range(total)]


def line_steps(own, size, coord, permute):
    if size != 4:
        for step in range(1, size):
            block = permute(own, lambda c, step=step: (c + step) % size)
            hold = yield
            yield hold(block)
        return
    even = lambda c: c ^ 1
    odd = lambda c: 3 - c if c in (1, 2) else None
    edge = jnp.logical_or(coord == 0, coord == 3)
    first, across = permute(own, even), permute(own, odd)
    hold = yield
    first, across = hold(first), hold(across)
    yield first
    ahead, over = permute(across, even), permute(first, odd)
    hold = yield
    ahead, over = hold(ahead), hold(over)
    yield jnp.where(edge, ahead, across)
    ahead = permute(over, even)
    hold = yield
    yield jnp.where(edge, hold(ahead), over)


def line_places(size, coord):
    if size != 4:
        return [coord] + [(coord + size - step) % size for step in range(1, size)]
    return [coord] + [
        jnp.where(coord == 0, a, jnp.where(coord == 1, b, jnp.where(coord == 2, c, d)))
        for a, b, c, d in ((1, 0, 3, 2), (2, 2, 1, 1), (3, 3, 0, 0))
    ]


def line_gather(own, size, coord, permute):
    found, steps = [own], line_steps(own, size, coord, permute)
    for _ in range(size - 1):
        next(steps)
        found.append(steps.send(lambda value: value))
    return found


def after(value, *others):
    anywhere = pl.BlockSpec(memory_space=pltpu.HBM)
    return pl.pallas_call(
        lambda *refs: None,
        out_shape=jax.ShapeDtypeStruct(value.shape, value.dtype),
        in_specs=[anywhere] * (1 + len(others)),
        out_specs=anywhere,
        input_output_aliases={0: 0},
        compiler_params=pltpu.CompilerParams(vmem_limit_bytes=VMEM_BYTES),
        cost_estimate=SMALL,
    )(value, *others)


def gated_scores(ids, chunks, own, blocks, parts, readout, carried):
    arrays, specs, scratch, shapes, copies = [], [], [], [], 0

    def add(array, space):
        for index, seen in enumerate(arrays):
            if seen is array:
                return index
        arrays.append(array)
        specs.append(pl.BlockSpec(memory_space=space))
        return len(arrays) - 1

    add(ids, pltpu.SMEM)
    small = []

    def add_small(array):
        small.append((add(array, pltpu.HBM), len(scratch)))
        scratch.append(pltpu.VMEM(array.shape, array.dtype))
        return small[-1][1]

    lines = own[1].shape[1]
    tiles, tile, width = own[0].shape
    place_count, block_rows = blocks[1].shape[0], blocks[1].shape[2]
    chunk_rows = chunks[0][2][0][0].shape[0]
    used_chunks = sorted({j for part in parts for j in range(part[3], part[4])})
    used_tiles = sorted({t for part in parts if part[0] for t in range(part[1], part[2])})
    used_blocks = sorted({t for part in parts if not part[0] for t in range(part[1], part[2])})
    lane_at, total_lanes = {}, 0
    for j in used_chunks:
        lane_at[j] = total_lanes
        total_lanes += 2 * chunks[j][1]
    weights_at = len(scratch)
    scratch.append(pltpu.VMEM((width, total_lanes), BF16))
    chunk_refs = {j: [(add(source[0], pltpu.HBM),) + source[1:] for source in chunks[j][2]] for j in used_chunks}
    copies += sum(len(refs) for refs in chunk_refs.values())
    own_at = block_at = own_out = block_out = None
    if used_tiles:
        own_at, own_out = len(scratch), len(shapes)
        scratch.append(pltpu.VMEM((len(used_tiles) * tile, width), BF16))
        shapes.append(jax.ShapeDtypeStruct((place_count, block_rows), F32))
        own_ref, own_lines, own_cols = add(own[0], pltpu.HBM), add_small(own[1]), add_small(own[2])
        copies += len(used_tiles)
    if used_blocks:
        block_at, block_out = len(scratch), len(shapes)
        scratch.append(pltpu.VMEM((len(used_blocks) * block_rows, width), BF16))
        shapes.append(jax.ShapeDtypeStruct((place_count, block_rows), F32))
        far_lines, far_cols = add_small(blocks[1]), add_small(blocks[2])
        block_refs = {n: [(add(array, pltpu.HBM), place) for array, place in blocks[0][n][1]] for n in used_blocks}
        copies += sum(len(refs) for refs in block_refs.values())
    sums_at = {}
    for mine, used, height in ((True, used_tiles, tile), (False, used_blocks, block_rows)):
        if used:
            sums_at[mine] = len(scratch)
            scratch.append(pltpu.VMEM((len(used) * height, 128), F32))
    readout_at = add_small(readout)
    carry = [
        (out, add_small(value)) for out, value in zip((own_out, block_out), carried) if out is not None and value is not None
    ]
    scratch.append(pltpu.SemaphoreType.DMA((copies + len(small),)))
    inputs, outputs = len(arrays), len(shapes)

    def kernel(*refs):
        ids_ref = refs[0]
        outs, held = refs[inputs : inputs + outputs], refs[inputs + outputs :]
        sems, readout_ref = held[-1], held[readout_at]
        pending, count = {}, 0

        def fetch(key):
            nonlocal count
            if key in pending:
                return
            pairs = []
            if key[0] == "chunk":
                for index, lane, shift, to, lanes, place in chunk_refs[key[1]]:
                    first = pl.multiple_of(ids_ref[place] * chunk_rows, chunk_rows)
                    if shift is not None:
                        lane = pl.multiple_of(ids_ref[shift] * 128 + lane, 128)
                    source = refs[index].at[:, pl.ds(lane, lanes)]
                    target = held[weights_at].at[pl.ds(first, chunk_rows), pl.ds(lane_at[key[1]] + to, lanes)]
                    pairs.append((source, target))
            elif key[0] == "own":
                rows = pl.ds(used_tiles.index(key[1]) * tile, tile)
                pairs.append((refs[own_ref].at[key[1]], held[own_at].at[rows, :]))
            else:
                for index, place in block_refs[key[1]]:
                    lanes = refs[index].shape[1]
                    first = pl.multiple_of(ids_ref[place] * lanes, lanes)
                    rows = pl.ds(used_blocks.index(key[1]) * block_rows, block_rows)
                    target = held[block_at].at[rows, pl.ds(first, lanes)]
                    pairs.append((refs[index], target))
            pending[key] = []
            for source, target in pairs:
                pending[key].append(pltpu.make_async_copy(source, target, sems.at[count]))
                pending[key][-1].start()
                count += 1

        def keys(part):
            mine, begin, end, first, last = part
            found = [("chunk", j) for j in range(first, last)]
            return found + [("own" if mine else "block", n) for n in range(begin, end)]

        first_copies = []
        for n, (index, place) in enumerate(small):
            first_copies.append(pltpu.make_async_copy(refs[index], held[place], sems.at[copies + n]))
            first_copies[-1].start()
        for part in parts[:2]:
            for key in keys(part):
                fetch(key)
        for n, out in enumerate(outs):
            if n not in dict(carry):
                out[...] = jnp.zeros(out.shape, F32)
        for copy in first_copies:
            copy.wait()
        for out, place in carry:
            outs[out][...] = held[place][...]
        summed = set()

        def add_line(mine, row, line):
            if not mine:
                outs[block_out][pl.ds(row, 1), :] += line
                return
            for k in range(tile // block_rows):
                at_row = row * (tile // block_rows) + k
                outs[own_out][at_row : at_row + 1, :] += line[:, k * block_rows : (k + 1) * block_rows]

        for number, part in enumerate(parts):
            for key in keys(part):
                for copy in pending[key]:
                    copy.wait()
                pending[key] = []
            if number + 2 < len(parts):
                for key in keys(parts[number + 2]):
                    fetch(key)
            mine, begin, end, first, last = part
            if mine:
                held_rows, height, at = held[own_at], tile, used_tiles.index(begin)
            else:
                held_rows, height, at = held[block_at], block_rows, used_blocks.index(begin)
            lanes = slice(lane_at[first], lane_at[last - 1] + 2 * chunks[last - 1][1])
            top, tall = at * height, (end - begin) * height
            piece = 240 if lanes.stop - lanes.start <= 256 and tall % 240 == 0 else tall
            pieces = [
                jnp.dot(held_rows[top + k : top + k + piece, :], held[weights_at][:, lanes], preferred_element_type=F32)
                for k in range(0, tall, piece)
            ]
            total = jnp.concatenate(pieces, 0) if len(pieces) > 1 else pieces[0]
            for t in range(end - begin):
                if mine:
                    row, noise, columns = begin + t, held[own_lines].at[begin + t], held[own_cols]
                else:
                    row = ids_ref[blocks[0][begin + t][0]]
                    noise, columns = held[far_lines].at[row], held[far_cols]
                begin_lane = 2 * chunks[first][0]
                part_total = total[t * height : (t + 1) * height, :] + lax.dot_general(
                    noise[...],
                    columns[:, begin_lane : begin_lane + lanes.stop - lanes.start],
                    (((0,), (0,)), ((), ())),
                    preferred_element_type=F32,
                )
                folded, lone = None, None
                for j in range(first, last):
                    start, size, _ = chunks[j]
                    lane = lane_at[j] - lane_at[first]
                    gate, up = part_total[:, lane : lane + size], part_total[:, lane + size : lane + 2 * size]
                    value = gate / (1.0 + jnp.exp(-gate)) * up * readout_ref[:, start : start + size]
                    if size % 128 == 0:
                        for k in range(0, size, 128):
                            block = value[:, k : k + 128]
                            folded = block if folded is None else folded + block
                    else:
                        line = jnp.sum(value.T, axis=0, keepdims=True)
                        lone = line if lone is None else lone + line
                if folded is not None:
                    there = held[sums_at[mine]].at[(at + t) * height : (at + t + 1) * height, :]
                    key = (mine, begin + t)
                    there[...] = folded + there[...] if key in summed else folded
                    summed.add(key)
                if lone is not None:
                    add_line(mine, row, lone)
        for mine, n in sorted(summed):
            height, used = (tile, used_tiles) if mine else (block_rows, used_blocks)
            value = held[sums_at[mine]][used.index(n) * height : (used.index(n) + 1) * height, :]
            row = n if mine else ids_ref[blocks[0][n][0]]
            add_line(mine, row, jnp.sum(value.T, axis=0, keepdims=True))

    results = pl.pallas_call(
        kernel,
        out_shape=shapes,
        in_specs=specs,
        out_specs=[pl.BlockSpec(memory_space=pltpu.VMEM)] * len(shapes),
        scratch_shapes=scratch,
        compiler_params=pltpu.CompilerParams(vmem_limit_bytes=VMEM_BYTES),
        cost_estimate=SMALL,
    )(*arrays)
    return (results[own_out] if used_tiles else carried[0]), (results[block_out] if used_blocks else carried[1])


def noise_columns(gate, up, cuts):
    blocks = []
    for begin, size in cuts:
        blocks += [gate[:, begin : begin + size], up[:, begin : begin + size]]
    value = jnp.concatenate(blocks, 1).astype(BF16)
    return jnp.concatenate([value] * 3, 0)


def lanes_from(ref, start, width, row=None):
    if start is None:
        return ref[...] if row is None else ref[row]
    lanes = pl.ds(pl.multiple_of(start * 128, 128), width)
    return ref[:, lanes] if row is None else ref[row, :, lanes]


def own_factors(starts, tokens, a_gate, a_up, gate_cols, up_cols, gate_half, up_half, fitness, scale, cuts, waited):
    members, tok_count, width = tokens.shape
    rank, hidden = a_gate.shape[1], gate_cols.shape[2]
    half, lines, block_half = hidden // 2, 2 * members * rank, width // 2
    halves = [] if gate_half is None else [gate_half, up_half]

    def kernel(starts_ref, tok_ref, ag, au, gc, uc, fit, waited_ref, *refs):
        bundle, rows, cols = refs[-3:]

        def both(gate, up):
            found = []
            for m in range(members):
                found += [gate(m).astype(F32), up(m).astype(F32)]
            return jnp.concatenate(found, 0).astype(BF16)

        bundle[:, :hidden] = both(lambda m: gc[m], lambda m: uc[m])
        bundle[:, hidden : hidden + block_half] = both(
            lambda m: lanes_from(ag, starts_ref[0], block_half, m), lambda m: lanes_from(au, starts_ref[0], block_half, m)
        )
        marks = [jnp.broadcast_to(fit[:, m : m + 1].astype(F32), (2 * rank, 128)) for m in range(members)]
        bundle[:, hidden + block_half : hidden + block_half + 128] = jnp.concatenate(marks, 0).astype(BF16)
        terms = []
        for m in range(members):
            factors = jnp.concatenate([ag[m].astype(F32), au[m].astype(F32)], 0).astype(BF16)
            value = scale * lax.dot_general(
                factors, tok_ref[m], (((1,), (1,)), ((), ())), preferred_element_type=F32
            )
            found = []
            for _ in range(3):
                found.append(value.astype(BF16).astype(F32))
                value = value - found[-1]
            terms.append(found)
            zero = jnp.zeros_like(value)
            lines_of = [found[n] if other == m else zero for n in range(3) for other in range(members)]
            rows[m] = jnp.concatenate(lines_of, 0).astype(BF16)
        ends = jnp.concatenate([jnp.concatenate(found, 1) for found in terms], 0)
        bundle[:, hidden + block_half + 128 :] = ends.astype(BF16)
        gates, ups = [], []
        for m in range(members):
            if halves:
                gate, up = refs[0][m].astype(F32), refs[1][m].astype(F32)
            else:
                gate = lanes_from(gc, starts_ref[1], half, m).astype(F32)
                up = lanes_from(uc, starts_ref[1], half, m).astype(F32)
            gates += [gate, jnp.zeros_like(gate)]
            ups += [jnp.zeros_like(up), up]
        cols[...] = noise_columns(jnp.concatenate(gates, 0), jnp.concatenate(ups, 0), cuts)

    vmem = pl.BlockSpec(memory_space=pltpu.VMEM)
    return pl.pallas_call(
        kernel,
        out_shape=[
            jax.ShapeDtypeStruct((lines, hidden + block_half + 128 + 3 * tok_count), BF16),
            jax.ShapeDtypeStruct((members, 3 * lines, tok_count), BF16),
            jax.ShapeDtypeStruct((3 * lines, 2 * half), BF16),
        ],
        in_specs=[pl.BlockSpec(memory_space=pltpu.SMEM)]
        + [vmem] * 6
        + [pl.BlockSpec(memory_space=pltpu.HBM)]
        + [vmem] * len(halves),
        out_specs=[vmem] * 3,
        compiler_params=pltpu.CompilerParams(vmem_limit_bytes=VMEM_BYTES),
        cost_estimate=SMALL,
    )(starts, tokens, a_gate, a_up, gate_cols, up_cols, fitness, waited, *halves)


def other_factors(starts, bundle, own_bundle, a_gate, a_up, half_cols, hidden, tok_count, tile, block_rows, cuts):
    members, rank, width = a_gate.shape
    lines, half, block_half = 2 * members * rank, hidden // 2, width // 2
    first = hidden + block_half + 128
    count, targets = members * tok_count // tile, (starts.shape[0] - 1) // 2
    halves = [] if half_cols is None else [half_cols]

    def kernel(starts_ref, bundle_ref, own_ref, ag, au, *refs):
        rows, cols = refs[len(halves) : len(halves) + 2]
        for block in range(count):
            m, at = block * tile // tok_count, block * tile % tok_count
            found = []
            for n in range(3):
                lane = first + n * tok_count + at
                value = bundle_ref[:, lane : lane + tile].astype(F32)
                line = lax.broadcasted_iota(jnp.int32, value.shape, 0)
                found.append(jnp.where(line // (2 * rank) == m, value, 0.0))
            rows[block] = jnp.concatenate(found, 0).astype(BF16)
        value = (refs[0][...] if halves else lanes_from(bundle_ref, starts_ref[0], half)).astype(F32)
        is_gate = lax.broadcasted_iota(jnp.int32, value.shape, 0) % (2 * rank) < rank
        cols[...] = noise_columns(jnp.where(is_gate, value, 0.0), jnp.where(is_gate, 0.0, value), cuts)
        for target in range(targets):
            pack = refs[len(halves) + 2 + target]
            pack[:lines, :hidden] = own_ref[:, :hidden]
            pack[lines:, :hidden] = bundle_ref[:, :hidden]
            mine = []
            for m in range(members):
                for source in (ag, au):
                    mine.append(lanes_from(source, starts_ref[2 + 2 * target], block_rows, m).astype(F32))
            pack[:lines, hidden : hidden + block_rows] = jnp.concatenate(mine, 0).astype(BF16)
            pack[lines:, hidden : hidden + block_rows] = lanes_from(
                bundle_ref, hidden // 128 + starts_ref[1 + 2 * target], block_rows
            )
            pack[:lines, hidden + block_rows :] = own_ref[:, first - 128 : first]
            pack[lines:, hidden + block_rows :] = bundle_ref[:, first - 128 : first]

    vmem = pl.BlockSpec(memory_space=pltpu.VMEM)
    return pl.pallas_call(
        kernel,
        out_shape=[
            jax.ShapeDtypeStruct((count, 3 * lines, tile), BF16),
            jax.ShapeDtypeStruct((3 * lines, 2 * half), BF16),
        ]
        + [jax.ShapeDtypeStruct((2 * lines, hidden + block_rows + 128), BF16)] * targets,
        in_specs=[pl.BlockSpec(memory_space=pltpu.SMEM)] + [vmem] * (4 + len(halves)),
        out_specs=[vmem] * (2 + targets),
        compiler_params=pltpu.CompilerParams(vmem_limit_bytes=VMEM_BYTES),
        cost_estimate=SMALL,
    )(starts, bundle, own_bundle, a_gate, a_up, *halves)


def update_directions(packs, hidden, block_rows, rank, total):
    step = 128

    def kernel(*refs):
        gate_out, up_out = refs[len(packs) :]
        lanes = pl.ds(pl.multiple_of(hidden + pl.program_id(0) * step, 128), step)
        left, right = [], []
        for ref in refs[: len(packs)]:
            value = ref[:, lanes].astype(F32) * (ref[:, hidden + block_rows : hidden + block_rows + 1].astype(F32) / math.sqrt(total))
            for _ in range(3):
                term = value.astype(BF16)
                left.append(term)
                value = value - term.astype(F32)
            right += [ref[:, :hidden]] * 3
        left, right = jnp.concatenate(left, 0), jnp.concatenate(right, 0)
        is_gate = lax.broadcasted_iota(jnp.int32, left.shape, 0) % (2 * rank) < rank
        for out, mask in ((gate_out, is_gate), (up_out, jnp.logical_not(is_gate))):
            part = jnp.where(mask, left.astype(F32), 0.0).astype(BF16)
            out[...] = lax.dot_general(part, right, (((0,), (0,)), ((), ())), preferred_element_type=F32)

    return pl.pallas_call(
        kernel,
        grid=(block_rows // step,),
        out_shape=[jax.ShapeDtypeStruct((block_rows, hidden), F32)] * 2,
        in_specs=[pl.BlockSpec(pack.shape, lambda i: (0, 0)) for pack in packs],
        out_specs=[pl.BlockSpec((step, hidden), lambda i: (i, 0))] * 2,
        compiler_params=pltpu.CompilerParams(vmem_limit_bytes=VMEM_BYTES),
        cost_estimate=SMALL,
    )(*packs)


def cut_blocks(gate, up, shift, groups, waited):
    rows = gate.shape[0]
    widths = [2 * sum(size for _, size in group) for group in groups]
    count = sum(2 * len(group) for group in groups)

    def kernel(shift_ref, gate_ref, up_ref, waited_ref, *refs):
        blocks, held, sems = refs[: len(groups)], refs[len(groups) : -1], refs[-1]
        first, used = [], 0
        for n, group in enumerate(groups):
            first.append([])
            for begin, size in group:
                lanes = pl.ds(pl.multiple_of(shift_ref[0] * 128 + begin, 128), size)
                to = 2 * (begin - group[0][0])
                for kind, source in enumerate((gate_ref, up_ref)):
                    target = held[n].at[:, pl.ds(to + kind * size, size)]
                    first[n].append(pltpu.make_async_copy(source.at[:, lanes], target, sems.at[used]))
                    first[n][-1].start()
                    used += 1
        second = []
        for n in range(len(groups)):
            for copy in first[n]:
                copy.wait()
            second.append(pltpu.make_async_copy(held[n], blocks[n], sems.at[used + n]))
            second[n].start()
        for copy in second:
            copy.wait()

    anywhere = pl.BlockSpec(memory_space=pltpu.HBM)
    return pl.pallas_call(
        kernel,
        out_shape=[jax.ShapeDtypeStruct((rows, width), gate.dtype) for width in widths],
        in_specs=[pl.BlockSpec(memory_space=pltpu.SMEM), anywhere, anywhere, anywhere],
        out_specs=[anywhere] * len(groups),
        scratch_shapes=[pltpu.VMEM((rows, width), gate.dtype) for width in widths]
        + [pltpu.SemaphoreType.DMA((count + len(groups),))],
        compiler_params=pltpu.CompilerParams(vmem_limit_bytes=VMEM_BYTES),
        cost_estimate=SMALL,
    )(shift, gate, up, waited)


def body(
    pop_size,
    shard_size,
    tokens,
    gate_weight_matrix,
    w_up,
    a_gate,
    a_up,
    gate_hidden_factors,
    up_hidden_factors,
    fitness,
    readout,
):
    members, tok_count, model_width = tokens.shape
    rank = a_gate.shape[1]
    rows = members * tok_count
    block_rows, hidden = gate_weight_matrix.shape
    half = hidden // 2
    lo_size = pop_size // 2
    outer, inner = line_sizes(shard_size)
    noise_scale = 0.25 / math.sqrt(model_width * rank)
    pop, shard = lax.axis_index("pop"), lax.axis_index("shard")
    hi, lo = pop // lo_size, pop % lo_size
    flat = tokens.reshape(rows, model_width)
    crossing = column_chunks(half)
    chunks = [chunk for group in crossing for chunk in group]

    across_pairs = [(p, (p + lo_size) % pop_size) for p in range(pop_size)]

    def across(value):
        return lax.ppermute(value, "pop", across_pairs)

    def along(value, step):
        pairs = [(p, p // lo_size * lo_size + (p + step) % lo_size) for p in range(pop_size)]
        return lax.ppermute(value, "pop", pairs)

    def outer_permute(value, target):
        pairs = [(s, target(s // inner), s % inner) for s in range(shard_size)]
        return lax.ppermute(value, "shard", [(s, z * inner + y) for s, z, y in pairs if z is not None])

    def inner_permute(value, target):
        pairs = [(s, s // inner, target(s % inner)) for s in range(shard_size)]
        return lax.ppermute(value, "shard", [(s, z * inner + y) for s, z, y in pairs if y is not None])

    z, y = shard // inner, shard % inner
    size_z, size_y = rows // outer, model_width // inner
    block = lax.dynamic_slice(flat, (z * size_z, y * size_y), (size_z, size_y))
    sent = across(block)

    block_half = model_width // 2
    by_start = half % 128 == 0

    def in_half(value):
        return None if by_start else lax.dynamic_slice_in_dim(value, hi * half, half, value.ndim - 1)

    def numbers(*values):
        return jnp.stack([jnp.asarray(value, jnp.int32) for value in values])

    half_start = hi * (half // 128)
    bundle, own_lines, own_columns = own_factors(
        numbers((1 - hi) * (block_half // 128), half_start),
        tokens,
        a_gate,
        a_up,
        gate_hidden_factors,
        up_hidden_factors,
        in_half(gate_hidden_factors),
        in_half(up_hidden_factors),
        fitness[None, :],
        noise_scale,
        chunks,
        block,
    )
    other_bundle = across(bundle)

    def pick(which):
        if half % 128 == 0:
            return cut_blocks(gate_weight_matrix, w_up, numbers(which * (half // 128)), crossing, bundle)
        gate = lax.dynamic_slice_in_dim(gate_weight_matrix, which * half, half, 1)
        up = lax.dynamic_slice_in_dim(w_up, which * half, half, 1)
        return [
            jnp.concatenate([part[:, begin : begin + size] for begin, size in group for part in (gate, up)], 1)
            for group in crossing
        ]

    cut = pick(1 - hi)
    if half % 128 == 0:
        near = [(along(gate_weight_matrix, step), along(w_up, step)) for step in range(1, lo_size)]
        near = [(gate_weight_matrix, w_up)] + near
    else:
        kept = jnp.concatenate(pick(hi), 1)
        near = [kept] + [along(kept, step) for step in range(1, lo_size)]

    sent = after(sent, other_bundle, *cut, *jax.tree.leaves(near[1:]))

    starts = [half_start]
    for step in range(lo_size):
        target = (lo + step) % lo_size
        starts += [target * (block_rows // 128), hi * (block_half // 128) + target * (block_rows // 128)]
    far_lines, far_columns, *packs = other_factors(
        numbers(*starts),
        other_bundle,
        bundle,
        a_gate,
        a_up,
        in_half(other_bundle[:, :hidden]),
        hidden,
        tok_count,
        size_z,
        block_rows,
        chunks,
    )
    packs = packs[:1] + [along(pack, step) for step, pack in enumerate(packs[1:], 1)]
    directions = update_directions(packs, hidden, block_rows, rank, pop_size * members * rank)

    half_readout = lax.dynamic_slice_in_dim(readout, hi * half, half, 0)[None, :]
    own = (tokens, own_lines, own_columns)
    held_at = pop_size + 1
    part_at = held_at + outer
    ids = numbers(
        *[hi * lo_size + (lo + lo_size - step) % lo_size for step in range(lo_size)],
        *[(1 - hi) * lo_size + (lo + lo_size - step) % lo_size for step in range(lo_size)],
        half_start,
        *line_places(outer, z),
        *line_places(inner, y),
    )

    steps = line_steps(sent, outer, z, outer_permute)
    held, spread, far, chunk_list = [sent], [line_gather(sent, inner, y, inner_permute)], [], []
    end = len(chunks)
    passed = [across(cut[0])] + [None] * (len(crossing) - 1)
    own_total = other_total = None
    done, barrier = [0] * outer, list(directions)

    def gather_next():
        next(steps)
        held.append(steps.send(lambda value: after(value, *barrier) if barrier else value))
        spread.append(line_gather(held[-1], inner, y, inner_permute))

    def bring(j):
        if passed[j] is None:
            passed[j] = across(after(cut[j], *(far[j - 2] if j > 1 else packs)))
        return passed[j]

    def score(parts):
        nonlocal own_total, other_total
        blocks = [
            (held_at + n, [(piece, part_at + k) for k, piece in enumerate(pieces)])
            for n, pieces in enumerate(spread)
        ]
        mine, theirs = gated_scores(
            ids, chunk_list, own, (blocks, far_lines, far_columns), parts, half_readout, (own_total, other_total)
        )
        own_total, other_total = mine, theirs
        return [value for value in (mine, theirs) if value is not None]

    for j, group in enumerate(crossing):
        block = bring(j)
        if len(held) < outer:
            recent = spread[-1][-1]
            gather_next()
            block = after(block, held[-1], recent)
        elif j:
            block = after(block, *barrier)
        far.append([block] + [along(block, step) for step in range(1, lo_size)])
        for begin, size in group:
            sources = []
            for n, kept_block in enumerate(near):
                if half % 128 == 0:
                    sources += [(value, begin, pop_size, k * size, size, n) for k, value in enumerate(kept_block)]
                else:
                    sources.append((kept_block, 2 * begin, None, 0, 2 * size, n))
            at = 2 * (begin - group[0][0])
            sources += [(value, at, None, 0, 2 * size, lo_size + n) for n, value in enumerate(far[j])]
            chunk_list.append((begin, size, sources))
        there = len(chunk_list)
        parts = [(True, t, t + 1, i, i + 1) for i in range(there - len(group), there) for t in range(members)]
        ready = min(j + 1, outer - 1)
        old = [n for n in range(ready) if done[n] == there - len(group)]
        for i in range(there - len(group), there):
            if old:
                parts.append((False, old[0], old[-1] + 1, i, i + 1))
        for n in range(ready):
            parts += [(False, n, n + 1, i, i + 1) for i in range(done[n], there) if n not in old]
            done[n] = there
        barrier = score(parts)
    while len(held) < outer:
        gather_next()
    rest = []
    for n in range(outer):
        cuts_at = list(range(done[n], max(done[n], end - 2))) + [max(done[n], end - 2), end]
        rest += [(False, n, n + 1, a, b) for a, b in zip(cuts_at, cuts_at[1:]) if a < b]
    near_own = [inner_permute(own_total, lambda c, s=s: (c + s) % inner) for s in range(1, inner)]
    if near_own:
        other_total = after(other_total, *near_own)
    score(rest)

    crossed = across(other_total)
    near_other = [
        lax.ppermute(
            other_total,
            ("pop", "shard"),
            [
                (p * shard_size + s, (p + lo_size) % pop_size * shard_size + s // inner * inner + (s + step) % inner)
                for p in range(pop_size)
                for s in range(shard_size)
            ],
        )
        for step in range(1, inner)
    ]
    scores = own_total + crossed + sum(near_own) + sum(near_other)
    scores = scores + sum(outer_permute(scores, lambda c, s=s: (c + s) % outer) for s in range(1, outer))
    return scores.reshape(members, tok_count), directions[0], directions[1]


def solution(mesh):
    placed = (
        P("pop", None, None),
        P("pop", "shard"),
        P("pop", "shard"),
        P("pop", None, None),
        P("pop", None, None),
        P("pop", None, "shard"),
        P("pop", None, "shard"),
        P("pop"),
        P("shard"),
    )
    return jax.shard_map(
        functools.partial(body, mesh.shape["pop"], mesh.shape["shard"]),
        mesh=mesh,
        in_specs=placed,
        out_specs=(P("pop", None), P("pop", "shard"), P("pop", "shard")),
        check_vma=False,
    )
```
